32 devices in a mesh: seq: 8 (over y, x, core), tp: 4 (over z).
Axes of the slice: x: 2, y: 2, z: 4, core: 2. Of those that a mesh axis runs over, the one named last changes fastest.
Arguments:
- query_rows: bfloat16 [2048, 6144], P('seq', 'tp'), may hold values from -6 to 6
- key_rows: bfloat16 [2048, 6144], P('seq', 'tp'), may hold values from -6 to 6
- value_rows: bfloat16 [2048, 6144], P('seq', 'tp'), may hold values from -6 to 6
- log_decay: float32 [48, 2048], P('tp', 'seq'), as said below
- doc_starts: int32 [8, 3], P('seq'), may hold values from 0 to 256, as said below
- residual_in: bfloat16 [2048, 4096], P(('seq', 'tp')), may hold values from -6 to 6
- out_weight: bfloat16 [6144, 4096], P('tp'), may hold values from -0.078125 to 0.078125
- norm_gain: float32 [4096], replicated, may hold values from 0.5 to 1.5
Outputs:
- hidden_state: bfloat16 [2048, 4096], P(('seq', 'tp'))
- normed_state: bfloat16 [2048, 4096], P(('seq', 'tp'))
The draws below stay inside these ranges and needn't reach their ends.
Inputs may be any that keep to these rules, and one draw needn't show every extreme that they name: `doc_starts`: each entry is a document's start offset within its shard; 256 marks an unused slot; the last entry of every row is 256; the first entry of shard 0 is 0; entries may repeat and need not be sorted. `log_decay`: every entry is negative.
All inputs are finite; a program needn't handle non-finite values.
Results may differ from the reference program's by a relative error of at most 0.022.
Values may be sent and summed in bfloat16 or wider, within the bound.
A program may use at most 64 MiB of HBM per device.

```python
import math
import jax
import jax.numpy as jnp
from jax import lax

D = 4096
HEADS_PER_SHARD = 48
HDIM = 128
SPAN = 256
MAXDOC = 3
SHARDS = 8
TOKEN_TOTAL = 2048
N_TP = 4


def draw_log_decay(key, part):
    key_entries = jax.random.split(key, 7)
    slow_rate = jnp.exp(jax.random.uniform(key_entries[0], (HEADS_PER_SHARD, 1), jnp.float32, math.log(0.1 / TOKEN_TOTAL), math.log(0.6 / TOKEN_TOTAL)))
    fast_rate = jnp.exp(jax.random.uniform(key_entries[1], (HEADS_PER_SHARD, 1), jnp.float32, math.log(0.004), math.log(0.05)))
    share = 0.5
    picked = jax.random.uniform(key_entries[2], (HEADS_PER_SHARD, 1), jnp.float32) < share
    decay_speed = jnp.where(picked, slow_rate, fast_rate)
    coarse_estimate = jnp.exp(jax.random.uniform(key_entries[3], (HEADS_PER_SHARD, TOKEN_TOTAL), jnp.float32, math.log(0.5), math.log(2.0)))
    block_list = jnp.exp(jax.random.uniform(key_entries[4], (HEADS_PER_SHARD, TOKEN_TOTAL // SPAN, 1), jnp.float32, math.log(0.5), math.log(2.0)))
    block_list = jnp.broadcast_to(block_list, (HEADS_PER_SHARD, TOKEN_TOTAL // SPAN, SPAN)).reshape(HEADS_PER_SHARD, TOKEN_TOTAL)
    sudden_jump = jax.random.uniform(key_entries[5], (HEADS_PER_SHARD, TOKEN_TOTAL), jnp.float32) < 3.0 / TOKEN_TOTAL
    decay_drop_amount = jnp.log(jax.random.uniform(key_entries[6], (HEADS_PER_SHARD, TOKEN_TOTAL), jnp.float32, 0.5, 0.8))
    return -(decay_speed * coarse_estimate * block_list) + jnp.where(sudden_jump, decay_drop_amount, 0.0)


def draw_doc_starts(key, part):
    raw = jax.random.randint(key, (SHARDS, MAXDOC - 1), 0, 8 * SPAN)
    picked = jnp.minimum(raw, SPAN).astype(jnp.int32)
    picked = picked.at[0, 0].set(0)
    unused = jnp.full((SHARDS, 1), SPAN, jnp.int32)
    return jnp.concatenate([picked, unused], axis=1)


def block_scale(own_key, extent, cuts, smallest, largest):
    gain = 1.0
    for dim, blocks in cuts:
        heights = jax.random.uniform(jax.random.fold_in(jax.random.fold_in(own_key, 6), dim), (blocks,), jnp.float32, smallest / len(cuts), largest / len(cuts))
        gain = gain * jnp.repeat(jnp.exp(heights), extent[dim] // blocks).reshape((-1,) + (1,) * (len(extent) - 1 - dim))
    return gain


def normal_values(own_key, shape, scale, bound, cuts=(), kind=jnp.bfloat16):
    entries = scale * jax.random.normal(own_key, shape, jnp.float32)
    if cuts:
        entries = entries * block_scale(own_key, shape, cuts, -0.22, 0.18)
    return jnp.clip(entries, -bound, bound).astype(kind)


def setup_inputs(seed: int = 0) -> dict:
    key_list = jax.random.split(jax.random.key(seed), 9)
    query_rows = normal_values(key_list[0], (TOKEN_TOTAL, HEADS_PER_SHARD * HDIM), 1.0, 6.0, ((0, 8), (1, 4)))
    key_rows = normal_values(key_list[1], (TOKEN_TOTAL, HEADS_PER_SHARD * HDIM), 1.0, 6.0, ((0, 8), (1, 4)))
    value_rows = normal_values(key_list[2], (TOKEN_TOTAL, HEADS_PER_SHARD * HDIM), 1.0, 6.0, ((0, 8), (1, 4)))
    log_decay = draw_log_decay(jax.random.fold_in(key_list[8], 71), 0)
    doc_starts = draw_doc_starts(jax.random.fold_in(key_list[8], 71), 0)
    residual_in = normal_values(key_list[5], (TOKEN_TOTAL, D), 1.0, 6.0, ((0, 32),))
    out_weight = normal_values(key_list[6], (HEADS_PER_SHARD * HDIM, D), (HEADS_PER_SHARD * HDIM) ** -0.5, 0.078125, ((0, 4),))
    norm_gain = jnp.clip(1.0 + 0.1 * jax.random.normal(key_list[7], (D,), jnp.float32), 0.5, 1.5)
    return {"query_rows": query_rows, "key_rows": key_rows, "value_rows": value_rows, "log_decay": log_decay, "doc_starts": doc_starts, "residual_in": residual_in, "out_weight": out_weight, "norm_gain": norm_gain}


def span_mix(query_c, key_c, value_c, decay_c, starts, state_in):
    length = query_c.shape[0]
    positions = jnp.arange(length, dtype=jnp.int32)
    segment = lax.optimization_barrier(jnp.sum((starts[None, :] <= positions[:, None]).astype(jnp.int32), axis=1))
    cumulative = jnp.cumsum(decay_c, axis=1)
    lower_mask = positions[:, None] >= positions[None, :]
    same_doc = lower_mask & (segment[:, None] == segment[None, :])
    spread = cumulative[:, :, None] - cumulative[:, None, :]
    decay_mat = jnp.exp(jnp.where(same_doc[None], spread, -jnp.inf))
    query_wide = query_c.astype(jnp.float32)
    key_wide = key_c.astype(jnp.float32)
    value_wide = value_c.astype(jnp.float32)
    scores = jnp.einsum('ihd,jhd->hij', query_wide, key_wide)
    weights = (scores * decay_mat).astype(jnp.bfloat16)
    intra_out = jnp.einsum('hij,jhd->ihd', weights.astype(jnp.float32), value_wide)
    first_doc = (segment == 0).astype(jnp.float32)
    carry_scale = jnp.exp(cumulative) * first_doc[None, :]
    state_low = state_in.astype(jnp.bfloat16).astype(jnp.float32)
    inter_out = jnp.einsum('ihd,hde->ihe', query_wide, state_low, precision=lax.Precision.HIGHEST) * carry_scale.T[:, :, None]
    last_seg = segment[length - 1]
    tail_weight = jnp.exp(cumulative[:, length - 1:] - cumulative) * (segment == last_seg).astype(jnp.float32)[None, :]
    decayed_keys = (key_wide * tail_weight.T[:, :, None]).astype(jnp.bfloat16).astype(jnp.float32)
    local_state = jnp.einsum('jhd,jhe->hde', decayed_keys, value_wide, precision=lax.Precision.HIGHEST)
    through = jnp.exp(cumulative[:, length - 1]) * (last_seg == 0).astype(jnp.float32)
    mixed = intra_out + inter_out
    normed = mixed * lax.rsqrt(lax.optimization_barrier(jnp.mean(mixed * mixed, axis=2, keepdims=True)) + 1e-06)
    return (normed.astype(jnp.bfloat16), through, local_state)

def reference(query_rows, key_rows, value_rows, log_decay, doc_starts, residual_in, out_weight, norm_gain):
    shards = TOKEN_TOTAL // SPAN
    heads_local = HEADS_PER_SHARD // N_TP
    query_all = query_rows.reshape(shards, SPAN, HEADS_PER_SHARD, HDIM)
    key_all = key_rows.reshape(shards, SPAN, HEADS_PER_SHARD, HDIM)
    value_all = value_rows.reshape(shards, SPAN, HEADS_PER_SHARD, HDIM)
    decay_all = log_decay.reshape(HEADS_PER_SHARD, shards, SPAN).transpose(1, 0, 2)

    def advance(state_in, inputs):
        query_c, key_c, value_c, decay_c, starts = inputs
        normed, through, local_state = span_mix(query_c, key_c, value_c, decay_c, starts, state_in)
        return (through[:, None, None] * state_in + local_state, normed)
    initial = jnp.zeros((HEADS_PER_SHARD, HDIM, HDIM), jnp.float32)
    final_state, attended = lax.scan(advance, initial, (query_all, key_all, value_all, decay_all, doc_starts))
    attended = attended.reshape(TOKEN_TOTAL, HEADS_PER_SHARD * HDIM)
    group_width = heads_local * HDIM
    summed = jnp.zeros((TOKEN_TOTAL, D), jnp.float32)
    for group in range(N_TP):
        piece = jnp.dot(attended[:, group * group_width:(group + 1) * group_width], out_weight[group * group_width:(group + 1) * group_width], preferred_element_type=jnp.float32).astype(jnp.bfloat16)
        summed = summed + piece.astype(jnp.float32)
    hidden = residual_in.astype(jnp.float32) + summed
    scale = lax.rsqrt(lax.optimization_barrier(jnp.mean(hidden * hidden, axis=1, keepdims=True)) + 1e-05)
    normed_state = (hidden * scale * norm_gain.astype(jnp.float32)[None, :]).astype(jnp.bfloat16)
    return (hidden.astype(jnp.bfloat16), normed_state)
```

```python
import functools

import jax
import jax.numpy as jnp
from jax import lax
from jax.experimental import pallas as pl
from jax.experimental.pallas import tpu as pltpu
from jax.sharding import PartitionSpec as P

MESH = pl.DeviceIdType.MESH
F32 = jnp.float32
BF16 = jnp.bfloat16
SKEW = 2


def _nt(a, b):
    return lax.dot_general(a, b, (((1,), (1,)), ((), ())), preferred_element_type=F32)


def _tn(a, b):
    return lax.dot_general(a, b, (((0,), (0,)), ((), ())), preferred_element_type=F32)


def kernel(
    cfg,
    q_ref, k_ref, v_ref, decay_ref, starts_ref, res_ref, gain_ref, w_hbm,
    hid_ref, norm_ref,
    wbuf, decay_pad, cum_rows, bias, cum_cols, carry_cols, intra, att,
    state_out, state_in, prefix_out, prefix_in,
    part, from_left, from_right, x_ref,
    w_sem, s1_send, s1_recv, s2_send, s2_recv, rs_send, left_recv, right_recv,
):
    ns, nt, heads, hd, span, m, chunks, width, rows = cfg
    per = hd // m
    body_rows = heads * per
    group = 3 if heads % 3 == 0 else 1
    me = lax.axis_index("seq")
    t = lax.axis_index("tp")

    def w_copy(c):
        return pltpu.make_async_copy(
            w_hbm.at[:, pl.ds(pl.multiple_of(c * width, width), width)], wbuf.at[c], w_sem.at[c]
        )

    for c in range(chunks):
        w_copy(c).start()

    barrier = pltpu.get_barrier_semaphore()
    for d in range(1, ns):
        pl.semaphore_signal(
            barrier, inc=1, device_id={"seq": lax.rem(me + d, ns)}, device_id_type=MESH
        )

    @pl.when(t > 0)
    def _():
        pl.semaphore_signal(barrier, inc=1, device_id={"tp": t - 1}, device_id_type=MESH)

    @pl.when(t < nt - 1)
    def _():
        pl.semaphore_signal(barrier, inc=1, device_id={"tp": t + 1}, device_id_type=MESH)

    row_i = lax.broadcasted_iota(jnp.int32, (span, span), 0)
    col_i = lax.broadcasted_iota(jnp.int32, (span, span), 1)
    lower = row_i >= col_i
    decay_pad[...] = jnp.zeros_like(decay_pad)
    decay_pad[0:heads, :] = decay_ref[...]
    cum = lax.dot_general(
        decay_pad[...], lower.astype(F32), (((1,), (1,)), ((), ())),
        preferred_element_type=F32, precision=lax.Precision.HIGHEST,
    )
    cum_rows[...] = cum
    cum_t = cum.T
    pos_c = lax.broadcasted_iota(jnp.int32, (span, 128), 0)
    seg_c = jnp.zeros((span, 128), jnp.int32)
    seg_r = jnp.zeros((1, span), jnp.int32)
    pos_r = lax.broadcasted_iota(jnp.int32, (1, span), 1)
    last_seg = jnp.zeros((1, 128), jnp.int32)
    for e in range(starts_ref.shape[1]):
        start = starts_ref[0, e]
        seg_c = seg_c + jnp.where(pos_c >= start, 1, 0)
        seg_r = seg_r + jnp.where(pos_r >= start, 1, 0)
        last_seg = last_seg + jnp.where(
            jnp.full((1, 128), span - 1, jnp.int32) >= start, 1, 0
        )
    tail_t = jnp.where(seg_c == last_seg, jnp.exp(cum_t[span - 1 : span, :] - cum_t), 0.0)
    carry_t = jnp.where(seg_c == 0, jnp.exp(cum_t), 0.0)

    for h in range(heads):
        lanes = slice(h * hd, (h + 1) * hd)
        dk = (k_ref[:, lanes].astype(F32) * tail_t[:, h : h + 1]).astype(BF16)
        local = _tn(dk, v_ref[:, lanes]).astype(BF16)
        for j in range(m):
            state_out[j, h * per : (h + 1) * per, :] = local[j * per : (j + 1) * per, :]
    through = jnp.where(last_seg == 0, jnp.exp(cum[:, span - 1 : span]), 0.0)[0:16, :]
    hi = through.astype(BF16)
    lo = (through - hi.astype(F32)).astype(BF16)
    for j in range(m):
        state_out[j, body_rows : body_rows + 16, :] = hi
        state_out[j, body_rows + 16 : body_rows + 32, :] = lo

    pl.semaphore_wait(
        barrier, ns - 1 + jnp.where(t > 0, 1, 0) + jnp.where(t < nt - 1, 1, 0)
    )

    def s1_copy(j, s):
        return pltpu.make_async_remote_copy(
            src_ref=state_out.at[j], dst_ref=state_in.at[s], send_sem=s1_send.at[j],
            recv_sem=s1_recv.at[s], device_id={"seq": j}, device_id_type=MESH,
        )

    def s2_copy(s, j):
        return pltpu.make_async_remote_copy(
            src_ref=prefix_out.at[s], dst_ref=prefix_in.at[j], send_sem=s2_send.at[s],
            recv_sem=s2_recv.at[j], device_id={"seq": s}, device_id_type=MESH,
        )

    for d in range(m):
        j = lax.rem(me + d, m)

        @pl.when((j != me) & (me < ns - 1))
        def _():
            s1_copy(j, me).start()

    @pl.when(me < m)
    def _():
        state_in[me] = state_out[me]

    seg_full = jnp.concatenate([seg_c] * (span // 128), axis=1)
    bias[...] = jnp.where(lower & (seg_full == seg_r), 0.0, -jnp.inf)
    for h in range(heads):
        cum_cols[h] = jnp.broadcast_to(cum_t[:, h : h + 1], (span, 128))
        carry_cols[h] = jnp.broadcast_to(carry_t[:, h : h + 1], (span, 128))

    def within(g, _):
        for o in range(group):
            h = g * group + o
            lanes = pl.ds(pl.multiple_of(h * hd, hd), hd)
            scores = _nt(q_ref[:, lanes], k_ref[:, lanes])
            cols = jnp.concatenate([cum_cols[h]] * (span // 128), axis=1)
            decay = jnp.exp(cols - cum_rows[pl.ds(h, 1), :] + bias[...])
            weights = (scores * decay).astype(BF16)
            intra[h] = jnp.dot(weights, v_ref[:, lanes], preferred_element_type=F32)
        return 0

    groups = heads // group
    lax.fori_loop(0, (groups + 1) // 2, within, 0)

    @pl.when(me < m)
    def _():
        state = [jnp.zeros((per, hd), F32) for _ in range(heads)]
        for s in range(ns - 1):

            @pl.when(me != s)
            def _():
                s1_copy(0, s).wait_recv()

            tail = state_in[s, body_rows : body_rows + 32, :].astype(F32)
            thr = tail[0:16] + tail[16:32]
            for h in range(heads):
                rows_h = slice(h * per, (h + 1) * per)
                state[h] = thr[h : h + 1, :] * state[h] + state_in[s, rows_h, :].astype(F32)
                prefix_out[s + 1, rows_h, :] = state[h].astype(BF16)

            @pl.when(me != s + 1)
            def _():
                s2_copy(s + 1, me).start()

        @pl.when(me > 0)
        def _():
            prefix_in[me] = prefix_out[me]

    lax.fori_loop((groups + 1) // 2, groups, within, 0)

    @pl.when(me == 0)
    def _():
        prefix_in[...] = jnp.zeros_like(prefix_in)

    for j in range(m):

        @pl.when((me > 0) & (me != j))
        def _():
            s2_copy(0, j).wait_recv()

    def across(g, _):
        for o in range(group):
            h = g * group + o
            lanes = pl.ds(pl.multiple_of(h * hd, hd), hd)
            rows_h = pl.ds(pl.multiple_of(h * per, per), per)
            state = jnp.concatenate([prefix_in[j, rows_h, :] for j in range(m)], axis=0)
            inter = jnp.dot(q_ref[:, lanes], state, preferred_element_type=F32)
            mixed = intra[h] + inter * carry_cols[h]
            mean = jnp.mean(mixed * mixed, axis=1, keepdims=True)
            att[:, lanes] = (mixed * lax.rsqrt(mean + 1e-06)).astype(BF16)
        return 0

    lax.fori_loop(0, groups, across, 0)

    def right_copy(b, c):
        return pltpu.make_async_remote_copy(
            src_ref=part.at[b, c], dst_ref=from_left.at[b, c], send_sem=rs_send.at[b, c],
            recv_sem=left_recv.at[b, c], device_id={"tp": jnp.minimum(t + 1, nt - 1)},
            device_id_type=MESH,
        )

    def left_copy(b, c):
        return pltpu.make_async_remote_copy(
            src_ref=part.at[b, c], dst_ref=from_right.at[b, c], send_sem=rs_send.at[b, c],
            recv_sem=right_recv.at[b, c], device_id={"tp": jnp.maximum(t - 1, 0)},
            device_id_type=MESH,
        )

    units = (nt - 1) * chunks

    def add_into(b, c, other):
        part[b, c] = (part[b, c].astype(F32) + other[b, c].astype(F32)).astype(BF16)

    def step(k, _):
        @pl.when(k < chunks)
        def _():
            w_copy(k).wait()
            out = jnp.dot(att[...], wbuf[k], preferred_element_type=F32).astype(BF16)
            for b in range(nt):
                part[b, k] = out[b * rows : (b + 1) * rows, :]

        ur = k - t * SKEW
        br = nt - 1 - ur // chunks
        cr = ur % chunks

        @pl.when((ur >= 0) & (ur < units) & (br > t))
        def _():
            @pl.when(t > 0)
            def _():
                right_copy(br, cr).wait_recv()
                add_into(br, cr, from_left)

            right_copy(br, cr).start()

        ul = k - (nt - 1 - t) * SKEW
        bl = ul // chunks
        cl = ul % chunks

        @pl.when((ul >= 0) & (ul < units) & (bl < t))
        def _():
            @pl.when(t < nt - 1)
            def _():
                left_copy(bl, cl).wait_recv()
                add_into(bl, cl, from_right)

            left_copy(bl, cl).start()

        return 0

    lax.fori_loop(0, units + (nt - 1) * SKEW, step, 0)

    total = jnp.zeros((rows, 1), F32)
    for c in range(chunks):
        lanes = slice(c * width, (c + 1) * width)
        x_ref[:, lanes] = res_ref[:, lanes].astype(F32) + part[t, c].astype(F32)

        @pl.when(t > 0)
        def _():
            right_copy(t, c).wait_recv()
            x_ref[:, lanes] += from_left[t, c].astype(F32)

        @pl.when(t < nt - 1)
        def _():
            left_copy(t, c).wait_recv()
            x_ref[:, lanes] += from_right[t, c].astype(F32)

        x = x_ref[:, lanes]
        hid_ref[:, lanes] = x.astype(BF16)
        total = total + jnp.sum(x * x, axis=1, keepdims=True)
    scale = lax.rsqrt(total / (chunks * width) + 1e-05)
    for c in range(chunks):
        lanes = slice(c * width, (c + 1) * width)
        norm_ref[:, lanes] = (x_ref[:, lanes] * scale * gain_ref[:, lanes]).astype(BF16)

    for j in range(m):

        @pl.when((me != j) & (me < ns - 1))
        def _():
            s1_copy(j, 0).wait_send()

    for s in range(1, ns):

        @pl.when((me != s) & (me < m))
        def _():
            s2_copy(s, 0).wait_send()

    def drain(u, _):
        b = u // chunks
        c = u % chunks

        @pl.when(b != t)
        def _():
            right_copy(b, c).wait_send()

        return 0

    lax.fori_loop(0, nt * chunks, drain, 0)


def shards(ns, nt, query, key, value, log_decay, doc_starts, residual, weight, gain):
    span = query.shape[0]
    heads = log_decay.shape[0]
    hd = query.shape[1] // heads
    rows, depth = residual.shape
    m = min(ns, hd // 16)
    per = hd // m
    chunks = 8
    width = depth // chunks
    cfg = (ns, nt, heads, hd, span, m, chunks, width, rows)
    vmem = pl.BlockSpec(memory_space=pltpu.VMEM)
    dma = pltpu.SemaphoreType.DMA
    return pl.pallas_call(
        functools.partial(kernel, cfg),
        out_shape=[jax.ShapeDtypeStruct((rows, depth), BF16)] * 2,
        in_specs=[vmem, vmem, vmem, vmem, pl.BlockSpec(memory_space=pltpu.SMEM), vmem, vmem,
                  pl.BlockSpec(memory_space=pl.ANY)],
        out_specs=[vmem, vmem],
        scratch_shapes=[
            pltpu.VMEM((chunks, weight.shape[0], width), BF16),
            pltpu.VMEM((128, span), F32),
            pltpu.VMEM((128, span), F32),
            pltpu.VMEM((span, span), F32),
            pltpu.VMEM((heads, span, 128), F32),
            pltpu.VMEM((heads, span, 128), F32),
            pltpu.VMEM((heads, span, hd), F32),
            pltpu.VMEM((span, heads * hd), BF16),
            pltpu.VMEM((m, heads * per + 32, hd), BF16),
            pltpu.VMEM((ns, heads * per + 32, hd), BF16),
            pltpu.VMEM((ns, heads * per, hd), BF16),
            pltpu.VMEM((m, heads * per, hd), BF16),
            pltpu.VMEM((nt, chunks, rows, width), BF16),
            pltpu.VMEM((nt, chunks, rows, width), BF16),
            pltpu.VMEM((nt, chunks, rows, width), BF16),
            pltpu.VMEM((rows, depth), F32),
            dma((chunks,)),
            dma((m,)),
            dma((ns,)),
            dma((ns,)),
            dma((m,)),
            dma((nt, chunks)),
            dma((nt, chunks)),
            dma((nt, chunks)),
        ],
        compiler_params=pltpu.CompilerParams(
            collective_id=0, has_side_effects=True, vmem_limit_bytes=56 * 1024 * 1024
        ),
        cost_estimate=pl.CostEstimate(
            flops=2 * span * weight.shape[0] * (depth + 4 * span),
            bytes_accessed=2 * weight.size + 6 * query.size + 6 * residual.size,
            transcendentals=heads * span * span,
        ),
    )(query, key, value, log_decay, doc_starts, residual, gain.reshape(1, depth), weight)


def solution(mesh):
    return jax.shard_map(
        functools.partial(shards, mesh.shape["seq"], mesh.shape["tp"]),
        mesh=mesh,
        in_specs=(
            P("seq", "tp"),
            P("seq", "tp"),
            P("seq", "tp"),
            P("tp", "seq"),
            P("seq", None),
            P(("seq", "tp"), None),
            P("tp", None),
            P(),
        ),
        out_specs=(P(("seq", "tp"), None), P(("seq", "tp"), None)),
        check_vma=False,
    )
```

```python
import functools

import jax
import jax.numpy as jnp
from jax import lax
from jax.experimental import pallas as pl
from jax.experimental.pallas import tpu as pltpu
from jax.sharding import PartitionSpec as P

MESH = pl.DeviceIdType.MESH
F32 = jnp.float32
BF16 = jnp.bfloat16
SKEW = 2


def _nt(a, b):
    return lax.dot_general(a, b, (((1,), (1,)), ((), ())), preferred_element_type=F32)


def _tn(a, b):
    return lax.dot_general(a, b, (((0,), (0,)), ((), ())), preferred_element_type=F32)


def kernel(
    cfg,
    q_hbm, k_hbm, v_hbm, decay_ref, starts_ref, res_hbm, w_hbm,
    x_hbm,
    q_ref, k_ref, v_ref, res_ref, wbuf, decay_pad, cum_rows, bias, cum_cols, carry_cols, intra, att,
    state_out, state_in, prefix_out, prefix_in,
    part, from_left, from_right, x_ref,
    in_sem, x_sem, w_sem, s1_send, s1_recv, s2_send, s2_recv, rs_send, left_recv, right_recv,
):
    ns, nt, heads, hd, span, m, chunks, width, rows = cfg
    per = hd // m
    sets = state_out.shape[0]
    set_heads = heads // sets
    body_rows = set_heads * per
    group = 3 if set_heads % 3 == 0 else 1
    me = lax.axis_index("seq")
    t = lax.axis_index("tp")

    loads = [
        pltpu.make_async_copy(src, dst, in_sem.at[i])
        for i, (src, dst) in enumerate(
            [(k_hbm, k_ref), (v_hbm, v_ref), (q_hbm, q_ref), (res_hbm, res_ref)]
        )
    ]
    for load in loads:
        load.start()

    def w_copy(c):
        return pltpu.make_async_copy(
            w_hbm.at[:, pl.ds(pl.multiple_of(c * width, width), width)], wbuf.at[c], w_sem.at[c]
        )

    barrier = pltpu.get_barrier_semaphore()
    for d in range(1, ns):
        pl.semaphore_signal(
            barrier, inc=1, device_id={"seq": lax.rem(me + d, ns)}, device_id_type=MESH
        )

    @pl.when(t > 0)
    def _():
        pl.semaphore_signal(barrier, inc=1, device_id={"tp": t - 1}, device_id_type=MESH)

    @pl.when(t < nt - 1)
    def _():
        pl.semaphore_signal(barrier, inc=1, device_id={"tp": t + 1}, device_id_type=MESH)

    row_i = lax.broadcasted_iota(jnp.int32, (span, span), 0)
    col_i = lax.broadcasted_iota(jnp.int32, (span, span), 1)
    lower = row_i >= col_i
    decay_pad[...] = jnp.zeros_like(decay_pad)
    decay_pad[0:heads, :] = decay_ref[...]
    cum = lax.dot_general(
        decay_pad[...], lower.astype(F32), (((1,), (1,)), ((), ())),
        preferred_element_type=F32, precision=lax.Precision.HIGHEST,
    )
    cum_rows[...] = cum
    cum_t = cum.T
    pos_c = lax.broadcasted_iota(jnp.int32, (span, 128), 0)
    seg_c = jnp.zeros((span, 128), jnp.int32)
    seg_r = jnp.zeros((1, span), jnp.int32)
    pos_r = lax.broadcasted_iota(jnp.int32, (1, span), 1)
    last_seg = jnp.zeros((1, 128), jnp.int32)
    for e in range(starts_ref.shape[1]):
        start = starts_ref[0, e]
        seg_c = seg_c + jnp.where(pos_c >= start, 1, 0)
        seg_r = seg_r + jnp.where(pos_r >= start, 1, 0)
        last_seg = last_seg + jnp.where(
            jnp.full((1, 128), span - 1, jnp.int32) >= start, 1, 0
        )
    tail_t = jnp.where(seg_c == last_seg, jnp.exp(cum_t[span - 1 : span, :] - cum_t), 0.0)
    carry_t = jnp.where(seg_c == 0, jnp.exp(cum_t), 0.0)

    through = jnp.where(last_seg == 0, jnp.exp(cum[:, span - 1 : span]), 0.0)[0:16, :]
    hi = through.astype(BF16)
    lo = (through - hi.astype(F32)).astype(BF16)

    def local_states(g):
        for i in range(set_heads):
            h = g * set_heads + i
            lanes = slice(h * hd, (h + 1) * hd)
            dk = (k_ref[:, lanes].astype(F32) * tail_t[:, h : h + 1]).astype(BF16)
            local = _tn(dk, v_ref[:, lanes]).astype(BF16)
            for j in range(m):
                state_out[g, j, i * per : (i + 1) * per, :] = local[j * per : (j + 1) * per, :]
        for j in range(m):
            state_out[g, j, body_rows : body_rows + 16, :] = hi
            state_out[g, j, body_rows + 16 : body_rows + 32, :] = lo

    def s1_copy(g, j, s):
        return pltpu.make_async_remote_copy(
            src_ref=state_out.at[g, j], dst_ref=state_in.at[g, s], send_sem=s1_send.at[g, j],
            recv_sem=s1_recv.at[g, s], device_id={"seq": j}, device_id_type=MESH,
        )

    def s2_copy(g, s, j):
        return pltpu.make_async_remote_copy(
            src_ref=prefix_out.at[g, s], dst_ref=prefix_in.at[g, j], send_sem=s2_send.at[g, s],
            recv_sem=s2_recv.at[g, j], device_id={"seq": s}, device_id_type=MESH,
        )

    def send_states(g):
        for d in range(m):
            j = lax.rem(me + d, m)

            @pl.when((j != me) & (me < ns - 1))
            def _():
                s1_copy(g, j, me).start()

        @pl.when(me < m)
        def _():
            state_in[g, me] = state_out[g, me]

    loads[0].wait()
    loads[1].wait()
    for c in range(chunks):
        w_copy(c).start()
    local_states(0)
    pl.semaphore_wait(
        barrier, ns - 1 + jnp.where(t > 0, 1, 0) + jnp.where(t < nt - 1, 1, 0)
    )
    send_states(0)
    for g in range(1, sets):
        local_states(g)
        send_states(g)

    seg_full = jnp.concatenate([seg_c] * (span // 128), axis=1)
    bias[...] = jnp.where(lower & (seg_full == seg_r), 0.0, -jnp.inf)
    for h in range(heads):
        cum_cols[h] = jnp.broadcast_to(cum_t[:, h : h + 1], (span, 128))
        carry_cols[h] = jnp.broadcast_to(carry_t[:, h : h + 1], (span, 128))
    loads[2].wait()

    def within(i, _):
        for o in range(group):
            h = i * group + o
            lanes = pl.ds(pl.multiple_of(h * hd, hd), hd)
            scores = _nt(q_ref[:, lanes], k_ref[:, lanes])
            cols = jnp.concatenate([cum_cols[h]] * (span // 128), axis=1)
            decay = jnp.exp(cols - cum_rows[pl.ds(h, 1), :] + bias[...])
            weights = (scores * decay).astype(BF16)
            intra[h] = jnp.dot(weights, v_ref[:, lanes], preferred_element_type=F32)
        return 0

    def scan(g):
        @pl.when(me < m)
        def _():
            state = [jnp.zeros((per, hd), F32) for _ in range(set_heads)]
            for s in range(ns - 1):

                @pl.when(me != s)
                def _():
                    s1_copy(g, 0, s).wait_recv()

                tail = state_in[g, s, body_rows : body_rows + 32, :].astype(F32)
                thr = tail[0:16] + tail[16:32]
                for i in range(set_heads):
                    h = g * set_heads + i
                    rows_h = slice(i * per, (i + 1) * per)
                    state[i] = thr[h : h + 1, :] * state[i] + state_in[g, s, rows_h, :].astype(F32)
                    prefix_out[g, s + 1, rows_h, :] = state[i].astype(BF16)

                @pl.when(me != s + 1)
                def _():
                    s2_copy(g, s + 1, me).start()

            @pl.when(me > 0)
            def _():
                prefix_in[g, me] = prefix_out[g, me]

        @pl.when(me == 0)
        def _():
            prefix_in[g] = jnp.zeros_like(prefix_in[g])

    def across(g):
        for j in range(m):

            @pl.when((me > 0) & (me != j))
            def _():
                s2_copy(g, 0, j).wait_recv()

        def some(n, _):
            for o in range(group):
                i = n * group + o
                h = g * set_heads + i
                lanes = pl.ds(pl.multiple_of(h * hd, hd), hd)
                rows_h = pl.ds(pl.multiple_of(i * per, per), per)
                state = jnp.concatenate([prefix_in[g, j, rows_h, :] for j in range(m)], axis=0)
                inter = jnp.dot(q_ref[:, lanes], state, preferred_element_type=F32)
                mixed = intra[h] + inter * carry_cols[h]
                mean = jnp.mean(mixed * mixed, axis=1, keepdims=True)
                att[:, lanes] = (mixed * lax.rsqrt(mean + 1e-06)).astype(BF16)
            return 0

        lax.fori_loop(0, set_heads // group, some, 0)

    per_set = set_heads // group
    for g in range(sets):
        lax.fori_loop(g * per_set, (g + 1) * per_set, within, 0)
        scan(g)
    for g in range(sets):
        across(g)

    def right_copy(b, c):
        return pltpu.make_async_remote_copy(
            src_ref=part.at[b, c], dst_ref=from_left.at[b, c], send_sem=rs_send.at[b, c],
            recv_sem=left_recv.at[b, c], device_id={"tp": jnp.minimum(t + 1, nt - 1)},
            device_id_type=MESH,
        )

    def left_copy(b, c):
        return pltpu.make_async_remote_copy(
            src_ref=part.at[b, c], dst_ref=from_right.at[b, c], send_sem=rs_send.at[b, c],
            recv_sem=right_recv.at[b, c], device_id={"tp": jnp.maximum(t - 1, 0)},
            device_id_type=MESH,
        )

    units = (nt - 1) * chunks

    def add_into(b, c, other):
        part[b, c] = (part[b, c].astype(F32) + other[b, c].astype(F32)).astype(BF16)

    def step(k, _):
        @pl.when(k < chunks)
        def _():
            w_copy(k).wait()
            out = jnp.dot(att[...], wbuf[k], preferred_element_type=F32).astype(BF16)
            for b in range(nt):
                part[b, k] = out[b * rows : (b + 1) * rows, :]

        ur = k - t * SKEW
        br = nt - 1 - ur // chunks
        cr = ur % chunks

        @pl.when((ur >= 0) & (ur < units) & (br > t))
        def _():
            @pl.when(t > 0)
            def _():
                right_copy(br, cr).wait_recv()
                add_into(br, cr, from_left)

            right_copy(br, cr).start()

        ul = k - (nt - 1 - t) * SKEW
        bl = ul // chunks
        cl = ul % chunks

        @pl.when((ul >= 0) & (ul < units) & (bl < t))
        def _():
            @pl.when(t < nt - 1)
            def _():
                left_copy(bl, cl).wait_recv()
                add_into(bl, cl, from_right)

            left_copy(bl, cl).start()

        return 0

    lax.fori_loop(0, units + (nt - 1) * SKEW, step, 0)

    loads[3].wait()

    def x_copy(c):
        return pltpu.make_async_copy(
            x_ref.at[c], x_hbm.at[:, pl.ds(c * width, width)], x_sem.at[c]
        )

    for c in range(chunks):
        lanes = slice(c * width, (c + 1) * width)
        x_ref[c] = res_ref[:, lanes].astype(F32) + part[t, c].astype(F32)

        @pl.when(t > 0)
        def _():
            right_copy(t, c).wait_recv()
            x_ref[c] += from_left[t, c].astype(F32)

        @pl.when(t < nt - 1)
        def _():
            left_copy(t, c).wait_recv()
            x_ref[c] += from_right[t, c].astype(F32)

        x_copy(c).start()
    for c in range(chunks):
        x_copy(c).wait()

    for g in range(sets):
        for j in range(m):

            @pl.when((me != j) & (me < ns - 1))
            def _():
                s1_copy(g, j, 0).wait_send()

        for s in range(1, ns):

            @pl.when((me != s) & (me < m))
            def _():
                s2_copy(g, s, 0).wait_send()

    def drain(u, _):
        b = u // chunks
        c = u % chunks

        @pl.when(b != t)
        def _():
            right_copy(b, c).wait_send()

        return 0

    lax.fori_loop(0, nt * chunks, drain, 0)


def norm_kernel(x_ref, gain_ref, hid_ref, norm_ref):
    x = x_ref[...]
    scale = lax.rsqrt(jnp.mean(x * x, axis=1, keepdims=True) + 1e-05)
    hid_ref[...] = x.astype(BF16)
    norm_ref[...] = (x * scale * gain_ref[...]).astype(BF16)


def shards(ns, nt, query, key, value, log_decay, doc_starts, residual, weight, gain):
    span = query.shape[0]
    heads = log_decay.shape[0]
    hd = query.shape[1] // heads
    rows, depth = residual.shape
    m = min(ns, hd // 16)
    per = hd // m
    sets = 2 if heads % 2 == 0 else 1
    body = heads // sets * per
    chunks = 8
    width = depth // chunks
    cfg = (ns, nt, heads, hd, span, m, chunks, width, rows)
    vmem = pl.BlockSpec(memory_space=pltpu.VMEM)
    hbm = pl.BlockSpec(memory_space=pl.ANY)
    dma = pltpu.SemaphoreType.DMA
    x = pl.pallas_call(
        functools.partial(kernel, cfg),
        out_shape=jax.ShapeDtypeStruct((rows, depth), F32),
        in_specs=[hbm, hbm, hbm, vmem, pl.BlockSpec(memory_space=pltpu.SMEM), hbm, hbm],
        out_specs=hbm,
        scratch_shapes=[
            pltpu.VMEM(query.shape, BF16),
            pltpu.VMEM(query.shape, BF16),
            pltpu.VMEM(query.shape, BF16),
            pltpu.VMEM(residual.shape, BF16),
            pltpu.VMEM((chunks, weight.shape[0], width), BF16),
            pltpu.VMEM((128, span), F32),
            pltpu.VMEM((128, span), F32),
            pltpu.VMEM((span, span), F32),
            pltpu.VMEM((heads, span, 128), F32),
            pltpu.VMEM((heads, span, 128), F32),
            pltpu.VMEM((heads, span, hd), F32),
            pltpu.VMEM((span, heads * hd), BF16),
            pltpu.VMEM((sets, m, body + 32, hd), BF16),
            pltpu.VMEM((sets, ns, body + 32, hd), BF16),
            pltpu.VMEM((sets, ns, body, hd), BF16),
            pltpu.VMEM((sets, m, body, hd), BF16),
            pltpu.VMEM((nt, chunks, rows, width), BF16),
            pltpu.VMEM((nt, chunks, rows, width), BF16),
            pltpu.VMEM((nt, chunks, rows, width), BF16),
            pltpu.VMEM((chunks, rows, width), F32),
            dma((4,)),
            dma((chunks,)),
            dma((chunks,)),
            dma((sets, m)),
            dma((sets, ns)),
            dma((sets, ns)),
            dma((sets, m)),
            dma((nt, chunks)),
            dma((nt, chunks)),
            dma((nt, chunks)),
        ],
        compiler_params=pltpu.CompilerParams(
            collective_id=0, has_side_effects=True, vmem_limit_bytes=56 * 1024 * 1024
        ),
        cost_estimate=pl.CostEstimate(
            flops=2 * span * weight.shape[0] * (depth + 4 * span),
            bytes_accessed=2 * weight.size + 6 * query.size + 6 * residual.size,
            transcendentals=heads * span * span,
        ),
    )(query, key, value, log_decay, doc_starts, residual, weight)
    block = pl.BlockSpec((16, depth), lambda i: (i, 0))
    return pl.pallas_call(
        norm_kernel,
        grid=(rows // 16,),
        out_shape=[jax.ShapeDtypeStruct((rows, depth), BF16)] * 2,
        in_specs=[block, pl.BlockSpec((1, depth), lambda i: (0, 0))],
        out_specs=[block, block],
        compiler_params=pltpu.CompilerParams(vmem_limit_bytes=56 * 1024 * 1024),
        cost_estimate=pl.CostEstimate(
            flops=6 * rows * depth, bytes_accessed=8 * rows * depth, transcendentals=rows
        ),
    )(x, gain.reshape(1, depth))


def solution(mesh):
    return jax.shard_map(
        functools.partial(shards, mesh.shape["seq"], mesh.shape["tp"]),
        mesh=mesh,
        in_specs=(
            P("seq", "tp"),
            P("seq", "tp"),
            P("seq", "tp"),
            P("tp", "seq"),
            P("seq", None),
            P(("seq", "tp"), None),
            P("tp", None),
            P(),
        ),
        out_specs=(P(("seq", "tp"), None), P(("seq", "tp"), None)),
        check_vma=False,
    )
```

```python
import functools

import jax
import jax.numpy as jnp
from jax import lax
from jax.experimental import pallas as pl
from jax.experimental.pallas import tpu as pltpu
from jax.sharding import PartitionSpec as P

MESH = pl.DeviceIdType.MESH
F32 = jnp.float32
BF16 = jnp.bfloat16
SKEW = 2


def _nt(a, b):
    return lax.dot_general(a, b, (((1,), (1,)), ((), ())), preferred_element_type=F32)


def _tn(a, b):
    return lax.dot_general(a, b, (((0,), (0,)), ((), ())), preferred_element_type=F32)


def kernel(
    cfg,
    q_hbm, k_hbm, v_hbm, decay_ref, starts_ref, res_hbm, gain_ref, w_hbm,
    hid_ref, norm_ref,
    q_ref, k_ref, v_ref, res_ref, wbuf, decay_pad, cum_rows, bias, cum_cols, carry_cols, intra, att,
    state_out, sibling_in, pair_out, pair_in, prefix_out, prefix_in, carried,
    part, from_left, from_right, x_ref,
    in_sem, w_sem, s0_send, s0_recv, s1_send, s1_recv, s2_send, s2_recv, s3_send, s3_recv, rs_send, left_recv, right_recv,
):
    ns, nt, heads, hd, span, m, chunks, width, rows = cfg
    per = hd // m
    sets = state_out.shape[0]
    set_heads = heads // sets
    body_rows = set_heads * per
    group = 3 if set_heads % 3 == 0 else 1
    me = lax.axis_index("seq")
    pairs, half = ns // 2, m // 2
    pair, core = me // 2, me % 2
    sibling = me + 1 - 2 * core
    t = lax.axis_index("tp")

    loads = [
        pltpu.make_async_copy(src, dst, in_sem.at[i])
        for i, (src, dst) in enumerate(
            [(k_hbm, k_ref), (v_hbm, v_ref), (q_hbm, q_ref), (res_hbm, res_ref)]
        )
    ]
    for load in loads:
        load.start()

    def w_copy(c):
        return pltpu.make_async_copy(
            w_hbm.at[:, pl.ds(pl.multiple_of(c * width, width), width)], wbuf.at[c], w_sem.at[c]
        )

    barrier = pltpu.get_barrier_semaphore()
    pl.semaphore_signal(barrier, inc=1, device_id={"seq": sibling}, device_id_type=MESH)
    for d in range(1, pairs):
        pl.semaphore_signal(
            barrier, inc=1, device_id={"seq": lax.rem(me + 2 * d, ns)}, device_id_type=MESH
        )

    @pl.when(t > 0)
    def _():
        pl.semaphore_signal(barrier, inc=1, device_id={"tp": t - 1}, device_id_type=MESH)

    @pl.when(t < nt - 1)
    def _():
        pl.semaphore_signal(barrier, inc=1, device_id={"tp": t + 1}, device_id_type=MESH)

    row_i = lax.broadcasted_iota(jnp.int32, (span, span), 0)
    col_i = lax.broadcasted_iota(jnp.int32, (span, span), 1)
    lower = row_i >= col_i
    decay_pad[...] = jnp.zeros_like(decay_pad)
    decay_pad[0:heads, :] = decay_ref[...]
    cum = lax.dot_general(
        decay_pad[...], lower.astype(F32), (((1,), (1,)), ((), ())),
        preferred_element_type=F32, precision=lax.Precision.HIGHEST,
    )
    cum_rows[...] = cum
    cum_t = cum.T
    pos_c = lax.broadcasted_iota(jnp.int32, (span, 128), 0)
    seg_c = jnp.zeros((span, 128), jnp.int32)
    seg_r = jnp.zeros((1, span), jnp.int32)
    pos_r = lax.broadcasted_iota(jnp.int32, (1, span), 1)
    last_seg = jnp.zeros((1, 128), jnp.int32)
    for e in range(starts_ref.shape[1]):
        start = starts_ref[0, e]
        seg_c = seg_c + jnp.where(pos_c >= start, 1, 0)
        seg_r = seg_r + jnp.where(pos_r >= start, 1, 0)
        last_seg = last_seg + jnp.where(
            jnp.full((1, 128), span - 1, jnp.int32) >= start, 1, 0
        )
    tail_t = jnp.where(seg_c == last_seg, jnp.exp(cum_t[span - 1 : span, :] - cum_t), 0.0)
    carry_t = jnp.where(seg_c == 0, jnp.exp(cum_t), 0.0)

    through = jnp.where(last_seg == 0, jnp.exp(cum[:, span - 1 : span]), 0.0)[0:16, :]
    hi = through.astype(BF16)
    lo = (through - hi.astype(F32)).astype(BF16)

    def local_states(g):
        for i in range(set_heads):
            h = g * set_heads + i
            lanes = slice(h * hd, (h + 1) * hd)
            dk = (k_ref[:, lanes].astype(F32) * tail_t[:, h : h + 1]).astype(BF16)
            local = _tn(dk, v_ref[:, lanes]).astype(BF16)
            for j in range(m):
                state_out[g, j % 2, j // 2, i * per : (i + 1) * per, :] = local[
                    j * per : (j + 1) * per, :
                ]
        for j in range(m):
            state_out[g, j % 2, j // 2, body_rows : body_rows + 16, :] = hi
            state_out[g, j % 2, j // 2, body_rows + 16 : body_rows + 32, :] = lo

    def s0_copy(g, whole):
        src, dst = state_out.at[g], sibling_in.at[g]
        return pltpu.make_async_remote_copy(
            src_ref=src if whole else src.at[0], dst_ref=dst if whole else dst.at[0],
            send_sem=s0_send.at[g], recv_sem=s0_recv.at[g],
            device_id={"seq": sibling}, device_id_type=MESH,
        )

    def s1_copy(g, i, p):
        return pltpu.make_async_remote_copy(
            src_ref=pair_out.at[g, i], dst_ref=pair_in.at[g, p], send_sem=s1_send.at[g, i],
            recv_sem=s1_recv.at[g, p], device_id={"seq": 2 * i + core}, device_id_type=MESH,
        )

    def s2_copy(g, p, i):
        return pltpu.make_async_remote_copy(
            src_ref=prefix_out.at[g, p], dst_ref=prefix_in.at[g, core, i],
            send_sem=s2_send.at[g, p], recv_sem=s2_recv.at[g, i],
            device_id={"seq": 2 * p + core}, device_id_type=MESH,
        )

    def s3_copy(g, c):
        return pltpu.make_async_remote_copy(
            src_ref=prefix_in.at[g, c], dst_ref=prefix_in.at[g, c], send_sem=s3_send.at[g],
            recv_sem=s3_recv.at[g], device_id={"seq": sibling}, device_id_type=MESH,
        )

    def send_states(g):
        @pl.when(core == 0)
        def _():
            s0_copy(g, True).start()

        @pl.when(core == 1)
        def _():
            s0_copy(g, False).start()

    def decays(block):
        tail = block[body_rows : body_rows + 32, :].astype(F32)
        return tail[0:16] + tail[16:32]

    def totals(g):
        def work(first, second, parity):
            thr0, thr1 = decays(first[g, parity, 0]), decays(second[g, parity, 0])
            both = thr0 * thr1
            both_hi = both.astype(BF16)
            both_lo = (both - both_hi.astype(F32)).astype(BF16)
            for d in range(half):
                for i in range(set_heads):
                    h = g * set_heads + i
                    rows_h = slice(i * per, (i + 1) * per)
                    pair_out[g, d, rows_h, :] = (
                        thr1[h : h + 1, :] * first[g, parity, d, rows_h, :].astype(F32)
                        + second[g, parity, d, rows_h, :].astype(F32)
                    ).astype(BF16)
                pair_out[g, d, body_rows : body_rows + 16, :] = both_hi
                pair_out[g, d, body_rows + 16 : body_rows + 32, :] = both_lo

        @pl.when(core == 0)
        def _():
            s0_copy(g, False).wait_recv()
            work(state_out, sibling_in, 0)

        @pl.when(core == 1)
        def _():
            s0_copy(g, True).wait_recv()
            work(sibling_in, state_out, 1)

        for d in range(half):
            i = lax.rem(pair + d, half)

            @pl.when((i != pair) & (pair < pairs - 1))
            def _():
                s1_copy(g, i, pair).start()

        @pl.when((pair < half) & (pair < pairs - 1))
        def _():
            pair_in[g, pair] = pair_out[g, pair]

    loads[0].wait()
    loads[1].wait()
    for c in range(chunks):
        w_copy(c).start()
    local_states(0)
    pl.semaphore_wait(
        barrier, pairs + jnp.where(t > 0, 1, 0) + jnp.where(t < nt - 1, 1, 0)
    )
    send_states(0)
    for g in range(1, sets):
        local_states(g)
        send_states(g)

    for g in range(sets):
        totals(g)

    seg_full = jnp.concatenate([seg_c] * (span // 128), axis=1)
    bias[...] = jnp.where(lower & (seg_full == seg_r), 0.0, -jnp.inf)
    for h in range(heads):
        cum_cols[h] = jnp.broadcast_to(cum_t[:, h : h + 1], (span, 128))
        carry_cols[h] = jnp.broadcast_to(carry_t[:, h : h + 1], (span, 128))
    loads[2].wait()

    def within(i, _):
        for o in range(group):
            h = i * group + o
            lanes = pl.ds(pl.multiple_of(h * hd, hd), hd)
            scores = _nt(q_ref[:, lanes], k_ref[:, lanes])
            cols = jnp.concatenate([cum_cols[h]] * (span // 128), axis=1)
            decay = jnp.exp(cols - cum_rows[pl.ds(h, 1), :] + bias[...])
            weights = (scores * decay).astype(BF16)
            intra[h] = jnp.dot(weights, v_ref[:, lanes], preferred_element_type=F32)
        return 0

    def scan(g):
        @pl.when(pair < half)
        def _():
            state = [jnp.zeros((per, hd), F32) for _ in range(set_heads)]
            for p in range(pairs - 1):

                @pl.when(pair != p)
                def _():
                    s1_copy(g, 0, p).wait_recv()

                thr = decays(pair_in[g, p])
                for i in range(set_heads):
                    h = g * set_heads + i
                    rows_h = slice(i * per, (i + 1) * per)
                    state[i] = thr[h : h + 1, :] * state[i] + pair_in[g, p, rows_h, :].astype(F32)
                    prefix_out[g, p + 1, rows_h, :] = state[i].astype(BF16)

                @pl.when(pair != p + 1)
                def _():
                    s2_copy(g, p + 1, pair).start()

            @pl.when(pair > 0)
            def _():
                prefix_in[g, core, pair] = prefix_out[g, pair]

        @pl.when(pair == 0)
        def _():
            prefix_in[g] = jnp.zeros_like(prefix_in[g])

    def share(g):
        @pl.when(pair > 0)
        def _():
            for i in range(half):

                @pl.when(pair != i)
                def _():
                    s2_copy(g, 0, i).wait_recv()

            s3_copy(g, core).start()

    def across(g):
        @pl.when(pair > 0)
        def _():
            s3_copy(g, 1 - core).wait_recv()

        @pl.when(core == 0)
        def _():
            for j in range(m):
                carried[g, j] = prefix_in[g, j % 2, j // 2]

        @pl.when(core == 1)
        def _():
            thr = decays(sibling_in[g, 0, 0])
            for j in range(m):
                for i in range(set_heads):
                    h = g * set_heads + i
                    rows_h = slice(i * per, (i + 1) * per)
                    carried[g, j, rows_h, :] = (
                        thr[h : h + 1, :] * prefix_in[g, j % 2, j // 2, rows_h, :].astype(F32)
                        + sibling_in[g, j % 2, j // 2, rows_h, :].astype(F32)
                    ).astype(BF16)

        def some(n, _):
            for o in range(group):
                i = n * group + o
                h = g * set_heads + i
                lanes = pl.ds(pl.multiple_of(h * hd, hd), hd)
                rows_h = pl.ds(pl.multiple_of(i * per, per), per)
                state = jnp.concatenate([carried[g, j, rows_h, :] for j in range(m)], axis=0)
                inter = jnp.dot(q_ref[:, lanes], state, preferred_element_type=F32)
                mixed = intra[h] + inter * carry_cols[h]
                mean = jnp.mean(mixed * mixed, axis=1, keepdims=True)
                att[:, lanes] = (mixed * lax.rsqrt(mean + 1e-06)).astype(BF16)
            return 0

        lax.fori_loop(0, set_heads // group, some, 0)

    per_set = set_heads // group
    lax.fori_loop(0, per_set, within, 0)
    for g in range(sets):
        scan(g)
    lax.fori_loop(per_set, sets * per_set, within, 0)
    for g in range(sets):
        share(g)
    for g in range(sets):
        across(g)

    def right_copy(b, c):
        return pltpu.make_async_remote_copy(
            src_ref=part.at[b, c], dst_ref=from_left.at[b, c], send_sem=rs_send.at[b, c],
            recv_sem=left_recv.at[b, c], device_id={"tp": jnp.minimum(t + 1, nt - 1)},
            device_id_type=MESH,
        )

    def left_copy(b, c):
        return pltpu.make_async_remote_copy(
            src_ref=part.at[b, c], dst_ref=from_right.at[b, c], send_sem=rs_send.at[b, c],
            recv_sem=right_recv.at[b, c], device_id={"tp": jnp.maximum(t - 1, 0)},
            device_id_type=MESH,
        )

    units = (nt - 1) * chunks

    def add_into(b, c, other):
        part[b, c] = (part[b, c].astype(F32) + other[b, c].astype(F32)).astype(BF16)

    def step(k, _):
        @pl.when(k < chunks)
        def _():
            w_copy(k).wait()
            out = jnp.dot(att[...], wbuf[k], preferred_element_type=F32).astype(BF16)
            for b in range(nt):
                part[b, k] = out[b * rows : (b + 1) * rows, :]

        ur = k - t * SKEW
        br = nt - 1 - ur // chunks
        cr = ur % chunks

        @pl.when((ur >= 0) & (ur < units) & (br > t))
        def _():
            @pl.when(t > 0)
            def _():
                right_copy(br, cr).wait_recv()
                add_into(br, cr, from_left)

            right_copy(br, cr).start()

        ul = k - (nt - 1 - t) * SKEW
        bl = ul // chunks
        cl = ul % chunks

        @pl.when((ul >= 0) & (ul < units) & (bl < t))
        def _():
            @pl.when(t < nt - 1)
            def _():
                left_copy(bl, cl).wait_recv()
                add_into(bl, cl, from_right)

            left_copy(bl, cl).start()

        return 0

    lax.fori_loop(0, units + (nt - 1) * SKEW, step, 0)

    loads[3].wait()

    total = jnp.zeros((rows, 1), F32)
    for c in range(chunks):
        lanes = slice(c * width, (c + 1) * width)
        x_ref[c] = res_ref[:, lanes].astype(F32) + part[t, c].astype(F32)

        @pl.when(t > 0)
        def _():
            right_copy(t, c).wait_recv()
            x_ref[c] += from_left[t, c].astype(F32)

        @pl.when(t < nt - 1)
        def _():
            left_copy(t, c).wait_recv()
            x_ref[c] += from_right[t, c].astype(F32)

        x = x_ref[c]
        hid_ref[:, lanes] = x.astype(BF16)
        total = total + jnp.sum(x * x, axis=1, keepdims=True)
    scale = lax.rsqrt(total / (chunks * width) + 1e-05)
    for c in range(chunks):
        lanes = slice(c * width, (c + 1) * width)
        norm_ref[:, lanes] = (x_ref[c] * scale * gain_ref[:, lanes]).astype(BF16)

    for g in range(sets):

        @pl.when(core == 0)
        def _():
            s0_copy(g, True).wait_send()

        @pl.when(core == 1)
        def _():
            s0_copy(g, False).wait_send()

        for i in range(half):

            @pl.when((pair != i) & (pair < pairs - 1))
            def _():
                s1_copy(g, i, 0).wait_send()

        for p in range(1, pairs):

            @pl.when((pair != p) & (pair < half))
            def _():
                s2_copy(g, p, 0).wait_send()

        @pl.when(pair > 0)
        def _():
            s3_copy(g, core).wait_send()

    def drain(u, _):
        b = u // chunks
        c = u % chunks

        @pl.when(b != t)
        def _():
            right_copy(b, c).wait_send()

        return 0

    lax.fori_loop(0, nt * chunks, drain, 0)


def shards(ns, nt, query, key, value, log_decay, doc_starts, residual, weight, gain):
    span = query.shape[0]
    heads = log_decay.shape[0]
    hd = query.shape[1] // heads
    rows, depth = residual.shape
    m = min(ns, hd // 16)
    pairs, half = ns // 2, m // 2
    per = hd // m
    sets = 2 if heads % 2 == 0 else 1
    body = heads // sets * per
    chunks = 8
    width = depth // chunks
    cfg = (ns, nt, heads, hd, span, m, chunks, width, rows)
    vmem = pl.BlockSpec(memory_space=pltpu.VMEM)
    hbm = pl.BlockSpec(memory_space=pl.ANY)
    dma = pltpu.SemaphoreType.DMA
    return pl.pallas_call(
        functools.partial(kernel, cfg),
        out_shape=[pltpu.VMEM((rows, depth), BF16)] * 2,
        in_specs=[hbm, hbm, hbm, vmem, pl.BlockSpec(memory_space=pltpu.SMEM), hbm, vmem, hbm],
        out_specs=[vmem, vmem],
        scratch_shapes=[
            pltpu.VMEM(query.shape, BF16),
            pltpu.VMEM(query.shape, BF16),
            pltpu.VMEM(query.shape, BF16),
            pltpu.VMEM(residual.shape, BF16),
            pltpu.VMEM((chunks, weight.shape[0], width), BF16),
            pltpu.VMEM((128, span), F32),
            pltpu.VMEM((128, span), F32),
            pltpu.VMEM((span, span), F32),
            pltpu.VMEM((heads, span, 128), F32),
            pltpu.VMEM((heads, span, 128), F32),
            pltpu.VMEM((heads, span, hd), F32),
            pltpu.VMEM((span, heads * hd), BF16),
            pltpu.VMEM((sets, 2, half, body + 32, hd), BF16),
            pltpu.VMEM((sets, 2, half, body + 32, hd), BF16),
            pltpu.VMEM((sets, half, body + 32, hd), BF16),
            pltpu.VMEM((sets, pairs, body + 32, hd), BF16),
            pltpu.VMEM((sets, pairs, body, hd), BF16),
            pltpu.VMEM((sets, 2, half, body, hd), BF16),
            pltpu.VMEM((sets, m, body, hd), BF16),
            pltpu.VMEM((nt, chunks, rows, width), BF16),
            pltpu.VMEM((nt, chunks, rows, width), BF16),
            pltpu.VMEM((nt, chunks, rows, width), BF16),
            pltpu.VMEM((chunks, rows, width), F32),
            dma((4,)),
            dma((chunks,)),
            dma((sets,)),
            dma((sets,)),
            dma((sets, half)),
            dma((sets, pairs)),
            dma((sets, pairs)),
            dma((sets, half)),
            dma((sets,)),
            dma((sets,)),
            dma((nt, chunks)),
            dma((nt, chunks)),
            dma((nt, chunks)),
        ],
        compiler_params=pltpu.CompilerParams(
            collective_id=0, has_side_effects=True, vmem_limit_bytes=56 * 1024 * 1024
        ),
        cost_estimate=pl.CostEstimate(
            flops=2 * span * weight.shape[0] * (depth + 4 * span),
            bytes_accessed=2 * weight.size + 6 * query.size + 6 * residual.size,
            transcendentals=heads * span * span,
        ),
    )(query, key, value, log_decay, doc_starts, residual, gain.reshape(1, depth), weight)


def solution(mesh):
    return jax.shard_map(
        functools.partial(shards, mesh.shape["seq"], mesh.shape["tp"]),
        mesh=mesh,
        in_specs=(
            P("seq", "tp"),
            P("seq", "tp"),
            P("seq", "tp"),
            P("tp", "seq"),
            P("seq", None),
            P(("seq", "tp"), None),
            P("tp", None),
            P(),
        ),
        out_specs=(P(("seq", "tp"), None), P(("seq", "tp"), None)),
        check_vma=False,
    )
```

```python
import functools

import jax
import jax.numpy as jnp
from jax import lax
from jax.experimental import pallas as pl
from jax.experimental.pallas import tpu as pltpu
from jax.sharding import PartitionSpec as P

MESH = pl.DeviceIdType.MESH
F32 = jnp.float32
BF16 = jnp.bfloat16
SKEW = 2


def _nt(a, b):
    return lax.dot_general(a, b, (((1,), (1,)), ((), ())), preferred_element_type=F32)


def _tn(a, b):
    return lax.dot_general(a, b, (((0,), (0,)), ((), ())), preferred_element_type=F32)


def kernel(
    cfg,
    q_hbm, k_hbm, v_hbm, decay_hbm, starts_hbm, res_hbm, gain_hbm, w_hbm,
    hid_ref, norm_ref,
    q_ref, k_ref, v_ref, decay_ref, starts_ref, res_ref, gain_ref, wbuf, decay_pad, cum_rows, bias, cum_cols, carry_cols, intra, att,
    state_out, sibling_in, pair_out, pair_in, prefix_out, prefix_in, carried,
    part, from_left, from_right, x_ref,
    in_sem, w_sem, s0_send, s0_recv, s1_send, s1_recv, s2_send, s2_recv, s3_send, s3_recv, rs_send, left_recv, right_recv,
):
    ns, nt, heads, hd, span, m, chunks, width, rows = cfg
    per = hd // m
    sets = state_out.shape[0]
    set_heads = heads // sets
    body_rows = set_heads * per
    group = 3 if set_heads % 3 == 0 else 1
    me = lax.axis_index("seq")
    pairs, half = ns // 2, m // 2
    pair, core = me // 2, me % 2
    sibling = me + 1 - 2 * core
    t = lax.axis_index("tp")

    pairs_of = [(decay_hbm, decay_ref), (starts_hbm, starts_ref)]
    for g in range(sets):
        lanes = pl.ds(g * set_heads * hd, set_heads * hd)
        pairs_of += [(k_hbm.at[:, lanes], k_ref.at[:, lanes]), (v_hbm.at[:, lanes], v_ref.at[:, lanes])]
    pairs_of += [(q_hbm, q_ref), (res_hbm, res_ref), (gain_hbm, gain_ref)]
    loads = [
        pltpu.make_async_copy(src, dst, in_sem.at[i]) for i, (src, dst) in enumerate(pairs_of)
    ]
    load_decay, load_starts, *load_sets, load_q, load_res, load_gain = loads
    for load in loads:
        load.start()

    def w_copy(c):
        return pltpu.make_async_copy(
            w_hbm.at[:, pl.ds(pl.multiple_of(c * width, width), width)], wbuf.at[c], w_sem.at[c]
        )

    barrier = pltpu.get_barrier_semaphore()
    pl.semaphore_signal(barrier, inc=1, device_id={"seq": sibling}, device_id_type=MESH)
    for d in range(1, pairs):
        pl.semaphore_signal(
            barrier, inc=1, device_id={"seq": lax.rem(me + 2 * d, ns)}, device_id_type=MESH
        )

    @pl.when(t > 0)
    def _():
        pl.semaphore_signal(barrier, inc=1, device_id={"tp": t - 1}, device_id_type=MESH)

    @pl.when(t < nt - 1)
    def _():
        pl.semaphore_signal(barrier, inc=1, device_id={"tp": t + 1}, device_id_type=MESH)

    row_i = lax.broadcasted_iota(jnp.int32, (span, span), 0)
    col_i = lax.broadcasted_iota(jnp.int32, (span, span), 1)
    lower = row_i >= col_i
    decay_pad[...] = jnp.zeros_like(decay_pad)
    load_decay.wait()
    decay_pad[0:heads, :] = decay_ref[...]
    cum = lax.dot_general(
        decay_pad[...], lower.astype(F32), (((1,), (1,)), ((), ())),
        preferred_element_type=F32, precision=lax.Precision.HIGHEST,
    )
    cum_rows[...] = cum
    cum_t = cum.T
    load_starts.wait()
    pos_c = lax.broadcasted_iota(jnp.int32, (span, 128), 0)
    seg_c = jnp.zeros((span, 128), jnp.int32)
    seg_r = jnp.zeros((1, span), jnp.int32)
    pos_r = lax.broadcasted_iota(jnp.int32, (1, span), 1)
    last_seg = jnp.zeros((1, 128), jnp.int32)
    for e in range(starts_ref.shape[1]):
        start = starts_ref[0, e]
        seg_c = seg_c + jnp.where(pos_c >= start, 1, 0)
        seg_r = seg_r + jnp.where(pos_r >= start, 1, 0)
        last_seg = last_seg + jnp.where(
            jnp.full((1, 128), span - 1, jnp.int32) >= start, 1, 0
        )
    tail_t = jnp.where(seg_c == last_seg, jnp.exp(cum_t[span - 1 : span, :] - cum_t), 0.0)
    carry_t = jnp.where(seg_c == 0, jnp.exp(cum_t), 0.0)

    through = jnp.where(last_seg == 0, jnp.exp(cum[:, span - 1 : span]), 0.0)[0:16, :]
    hi = through.astype(BF16)
    lo = (through - hi.astype(F32)).astype(BF16)

    def local_states(g):
        for i in range(set_heads):
            h = g * set_heads + i
            lanes = slice(h * hd, (h + 1) * hd)
            dk = (k_ref[:, lanes].astype(F32) * tail_t[:, h : h + 1]).astype(BF16)
            local = _tn(dk, v_ref[:, lanes]).astype(BF16)
            for j in range(m):
                state_out[g, j % 2, j // 2, i * per : (i + 1) * per, :] = local[
                    j * per : (j + 1) * per, :
                ]
        for j in range(m):
            state_out[g, j % 2, j // 2, body_rows : body_rows + 16, :] = hi
            state_out[g, j % 2, j // 2, body_rows + 16 : body_rows + 32, :] = lo

    def s0_copy(g, whole):
        src, dst = state_out.at[g], sibling_in.at[g]
        return pltpu.make_async_remote_copy(
            src_ref=src if whole else src.at[0], dst_ref=dst if whole else dst.at[0],
            send_sem=s0_send.at[g], recv_sem=s0_recv.at[g],
            device_id={"seq": sibling}, device_id_type=MESH,
        )

    def s1_copy(g, i, p):
        return pltpu.make_async_remote_copy(
            src_ref=pair_out.at[g, i], dst_ref=pair_in.at[g, p], send_sem=s1_send.at[g, i],
            recv_sem=s1_recv.at[g, p], device_id={"seq": 2 * i + core}, device_id_type=MESH,
        )

    def s2_copy(g, p, i):
        return pltpu.make_async_remote_copy(
            src_ref=prefix_out.at[g, p], dst_ref=prefix_in.at[g, core, i],
            send_sem=s2_send.at[g, p], recv_sem=s2_recv.at[g, i],
            device_id={"seq": 2 * p + core}, device_id_type=MESH,
        )

    def s3_copy(g, c):
        return pltpu.make_async_remote_copy(
            src_ref=prefix_in.at[g, c], dst_ref=prefix_in.at[g, c], send_sem=s3_send.at[g],
            recv_sem=s3_recv.at[g], device_id={"seq": sibling}, device_id_type=MESH,
        )

    def send_states(g):
        @pl.when(core == 0)
        def _():
            s0_copy(g, True).start()

        @pl.when(core == 1)
        def _():
            s0_copy(g, False).start()

    def decays(block):
        tail = block[body_rows : body_rows + 32, :].astype(F32)
        return tail[0:16] + tail[16:32]

    def totals(g):
        def work(first, second, parity):
            thr0, thr1 = decays(first[g, parity, 0]), decays(second[g, parity, 0])
            both = thr0 * thr1
            both_hi = both.astype(BF16)
            both_lo = (both - both_hi.astype(F32)).astype(BF16)
            for d in range(half):
                for i in range(set_heads):
                    h = g * set_heads + i
                    rows_h = slice(i * per, (i + 1) * per)
                    pair_out[g, d, rows_h, :] = (
                        thr1[h : h + 1, :] * first[g, parity, d, rows_h, :].astype(F32)
                        + second[g, parity, d, rows_h, :].astype(F32)
                    ).astype(BF16)
                pair_out[g, d, body_rows : body_rows + 16, :] = both_hi
                pair_out[g, d, body_rows + 16 : body_rows + 32, :] = both_lo

        @pl.when(core == 0)
        def _():
            s0_copy(g, False).wait_recv()
            work(state_out, sibling_in, 0)

        @pl.when(core == 1)
        def _():
            s0_copy(g, True).wait_recv()
            work(sibling_in, state_out, 1)

        for d in range(half):
            i = lax.rem(pair + d, half)

            @pl.when((i != pair) & (pair < pairs - 1))
            def _():
                s1_copy(g, i, pair).start()

        @pl.when((pair < half) & (pair < pairs - 1))
        def _():
            pair_in[g, pair] = pair_out[g, pair]

    for load in load_sets[0:2]:
        load.wait()
    local_states(0)
    pl.semaphore_wait(
        barrier, pairs + jnp.where(t > 0, 1, 0) + jnp.where(t < nt - 1, 1, 0)
    )
    send_states(0)
    for load in load_sets[2:]:
        load.wait()
    for c in range(chunks):
        w_copy(c).start()
    for g in range(1, sets):
        local_states(g)
        send_states(g)

    for g in range(sets):
        totals(g)

    seg_full = jnp.concatenate([seg_c] * (span // 128), axis=1)
    bias[...] = jnp.where(lower & (seg_full == seg_r), 0.0, -jnp.inf)
    for h in range(heads):
        cum_cols[h] = jnp.broadcast_to(cum_t[:, h : h + 1], (span, 128))
        carry_cols[h] = jnp.broadcast_to(carry_t[:, h : h + 1], (span, 128))
    load_q.wait()

    def within(i, _):
        for o in range(group):
            h = i * group + o
            lanes = pl.ds(pl.multiple_of(h * hd, hd), hd)
            scores = _nt(q_ref[:, lanes], k_ref[:, lanes])
            cols = jnp.concatenate([cum_cols[h]] * (span // 128), axis=1)
            decay = jnp.exp(cols - cum_rows[pl.ds(h, 1), :] + bias[...])
            weights = (scores * decay).astype(BF16)
            intra[h] = jnp.dot(weights, v_ref[:, lanes], preferred_element_type=F32)
        return 0

    def scan(g):
        @pl.when(pair < half)
        def _():
            state = [jnp.zeros((per, hd), F32) for _ in range(set_heads)]
            for p in range(pairs - 1):

                @pl.when(pair != p)
                def _():
                    s1_copy(g, 0, p).wait_recv()

                thr = decays(pair_in[g, p])
                for i in range(set_heads):
                    h = g * set_heads + i
                    rows_h = slice(i * per, (i + 1) * per)
                    state[i] = thr[h : h + 1, :] * state[i] + pair_in[g, p, rows_h, :].astype(F32)
                    prefix_out[g, p + 1, rows_h, :] = state[i].astype(BF16)

                @pl.when(pair != p + 1)
                def _():
                    s2_copy(g, p + 1, pair).start()

            @pl.when(pair > 0)
            def _():
                prefix_in[g, core, pair] = prefix_out[g, pair]

        @pl.when(pair == 0)
        def _():
            prefix_in[g] = jnp.zeros_like(prefix_in[g])

    def share(g):
        @pl.when(pair > 0)
        def _():
            for i in range(half):

                @pl.when(pair != i)
                def _():
                    s2_copy(g, 0, i).wait_recv()

            s3_copy(g, core).start()

    def across(g):
        @pl.when(pair > 0)
        def _():
            s3_copy(g, 1 - core).wait_recv()

        @pl.when(core == 0)
        def _():
            for j in range(m):
                carried[g, j] = prefix_in[g, j % 2, j // 2]

        @pl.when(core == 1)
        def _():
            thr = decays(sibling_in[g, 0, 0])
            for j in range(m):
                for i in range(set_heads):
                    h = g * set_heads + i
                    rows_h = slice(i * per, (i + 1) * per)
                    carried[g, j, rows_h, :] = (
                        thr[h : h + 1, :] * prefix_in[g, j % 2, j // 2, rows_h, :].astype(F32)
                        + sibling_in[g, j % 2, j // 2, rows_h, :].astype(F32)
                    ).astype(BF16)

        def some(n, _):
            for o in range(group):
                i = n * group + o
                h = g * set_heads + i
                lanes = pl.ds(pl.multiple_of(h * hd, hd), hd)
                rows_h = pl.ds(pl.multiple_of(i * per, per), per)
                state = jnp.concatenate([carried[g, j, rows_h, :] for j in range(m)], axis=0)
                inter = jnp.dot(q_ref[:, lanes], state, preferred_element_type=F32)
                mixed = intra[h] + inter * carry_cols[h]
                mean = jnp.mean(mixed * mixed, axis=1, keepdims=True)
                att[:, lanes] = (mixed * lax.rsqrt(mean + 1e-06)).astype(BF16)
            return 0

        lax.fori_loop(0, set_heads // group, some, 0)

    per_set = set_heads // group
    lax.fori_loop(0, per_set, within, 0)
    for g in range(sets):
        scan(g)
    lax.fori_loop(per_set, sets * per_set, within, 0)
    for g in range(sets):
        share(g)
    for g in range(sets):
        across(g)

    def right_copy(b, c):
        return pltpu.make_async_remote_copy(
            src_ref=part.at[b, c], dst_ref=from_left.at[b, c], send_sem=rs_send.at[b, c],
            recv_sem=left_recv.at[b, c], device_id={"tp": jnp.minimum(t + 1, nt - 1)},
            device_id_type=MESH,
        )

    def left_copy(b, c):
        return pltpu.make_async_remote_copy(
            src_ref=part.at[b, c], dst_ref=from_right.at[b, c], send_sem=rs_send.at[b, c],
            recv_sem=right_recv.at[b, c], device_id={"tp": jnp.maximum(t - 1, 0)},
            device_id_type=MESH,
        )

    units = (nt - 1) * chunks

    def add_into(b, c, other):
        part[b, c] = (part[b, c].astype(F32) + other[b, c].astype(F32)).astype(BF16)

    def step(k, _):
        @pl.when(k < chunks)
        def _():
            w_copy(k).wait()
            out = jnp.dot(att[...], wbuf[k], preferred_element_type=F32).astype(BF16)
            for b in range(nt):
                part[b, k] = out[b * rows : (b + 1) * rows, :]

        ur = k - t * SKEW
        br = nt - 1 - ur // chunks
        cr = ur % chunks

        @pl.when((ur >= 0) & (ur < units) & (br > t))
        def _():
            @pl.when(t > 0)
            def _():
                right_copy(br, cr).wait_recv()
                add_into(br, cr, from_left)

            right_copy(br, cr).start()

        ul = k - (nt - 1 - t) * SKEW
        bl = ul // chunks
        cl = ul % chunks

        @pl.when((ul >= 0) & (ul < units) & (bl < t))
        def _():
            @pl.when(t < nt - 1)
            def _():
                left_copy(bl, cl).wait_recv()
                add_into(bl, cl, from_right)

            left_copy(bl, cl).start()

        return 0

    lax.fori_loop(0, units + (nt - 1) * SKEW, step, 0)

    load_res.wait()
    load_gain.wait()

    total = jnp.zeros((rows, 1), F32)
    for c in range(chunks):
        lanes = slice(c * width, (c + 1) * width)
        x_ref[c] = res_ref[:, lanes].astype(F32) + part[t, c].astype(F32)

        @pl.when(t > 0)
        def _():
            right_copy(t, c).wait_recv()
            x_ref[c] += from_left[t, c].astype(F32)

        @pl.when(t < nt - 1)
        def _():
            left_copy(t, c).wait_recv()
            x_ref[c] += from_right[t, c].astype(F32)

        x = x_ref[c]
        hid_ref[:, lanes] = x.astype(BF16)
        total = total + jnp.sum(x * x, axis=1, keepdims=True)
    scale = lax.rsqrt(total / (chunks * width) + 1e-05)
    for c in range(chunks):
        lanes = slice(c * width, (c + 1) * width)
        norm_ref[:, lanes] = (x_ref[c] * scale * gain_ref[:, lanes]).astype(BF16)

    for g in range(sets):

        @pl.when(core == 0)
        def _():
            s0_copy(g, True).wait_send()

        @pl.when(core == 1)
        def _():
            s0_copy(g, False).wait_send()

        for i in range(half):

            @pl.when((pair != i) & (pair < pairs - 1))
            def _():
                s1_copy(g, i, 0).wait_send()

        for p in range(1, pairs):

            @pl.when((pair != p) & (pair < half))
            def _():
                s2_copy(g, p, 0).wait_send()

        @pl.when(pair > 0)
        def _():
            s3_copy(g, core).wait_send()

    def drain(u, _):
        b = u // chunks
        c = u % chunks

        @pl.when(b != t)
        def _():
            right_copy(b, c).wait_send()

        return 0

    lax.fori_loop(0, nt * chunks, drain, 0)


def write_kernel(hid_ref, norm_ref, hid_hbm, norm_hbm, sem):
    copies = [
        pltpu.make_async_copy(hid_ref, hid_hbm, sem.at[0]),
        pltpu.make_async_copy(norm_ref, norm_hbm, sem.at[1]),
    ]
    for copy in copies:
        copy.start()
    for copy in copies:
        copy.wait()


def shards(ns, nt, query, key, value, log_decay, doc_starts, residual, weight, gain):
    span = query.shape[0]
    heads = log_decay.shape[0]
    hd = query.shape[1] // heads
    rows, depth = residual.shape
    m = min(ns, hd // 16)
    pairs, half = ns // 2, m // 2
    per = hd // m
    sets = 2 if heads % 2 == 0 else 1
    body = heads // sets * per
    chunks = 8
    width = depth // chunks
    cfg = (ns, nt, heads, hd, span, m, chunks, width, rows)
    vmem = pl.BlockSpec(memory_space=pltpu.VMEM)
    hbm = pl.BlockSpec(memory_space=pl.ANY)
    dma = pltpu.SemaphoreType.DMA
    outs = pl.pallas_call(
        functools.partial(kernel, cfg),
        out_shape=[pltpu.VMEM((rows, depth), BF16)] * 2,
        in_specs=[hbm] * 8,
        out_specs=[vmem, vmem],
        scratch_shapes=[
            pltpu.VMEM(query.shape, BF16),
            pltpu.VMEM(query.shape, BF16),
            pltpu.VMEM(query.shape, BF16),
            pltpu.VMEM(log_decay.shape, F32),
            pltpu.SMEM(doc_starts.shape, jnp.int32),
            pltpu.VMEM(residual.shape, BF16),
            pltpu.VMEM((1, depth), F32),
            pltpu.VMEM((chunks, weight.shape[0], width), BF16),
            pltpu.VMEM((128, span), F32),
            pltpu.VMEM((128, span), F32),
            pltpu.VMEM((span, span), F32),
            pltpu.VMEM((heads, span, 128), F32),
            pltpu.VMEM((heads, span, 128), F32),
            pltpu.VMEM((heads, span, hd), F32),
            pltpu.VMEM((span, heads * hd), BF16),
            pltpu.VMEM((sets, 2, half, body + 32, hd), BF16),
            pltpu.VMEM((sets, 2, half, body + 32, hd), BF16),
            pltpu.VMEM((sets, half, body + 32, hd), BF16),
            pltpu.VMEM((sets, pairs, body + 32, hd), BF16),
            pltpu.VMEM((sets, pairs, body, hd), BF16),
            pltpu.VMEM((sets, 2, half, body, hd), BF16),
            pltpu.VMEM((sets, m, body, hd), BF16),
            pltpu.VMEM((nt, chunks, rows, width), BF16),
            pltpu.VMEM((nt, chunks, rows, width), BF16),
            pltpu.VMEM((nt, chunks, rows, width), BF16),
            pltpu.VMEM((chunks, rows, width), F32),
            dma((5 + 2 * sets,)),
            dma((chunks,)),
            dma((sets,)),
            dma((sets,)),
            dma((sets, half)),
            dma((sets, pairs)),
            dma((sets, pairs)),
            dma((sets, half)),
            dma((sets,)),
            dma((sets,)),
            dma((nt, chunks)),
            dma((nt, chunks)),
            dma((nt, chunks)),
        ],
        compiler_params=pltpu.CompilerParams(
            collective_id=0, has_side_effects=True, vmem_limit_bytes=56 * 1024 * 1024
        ),
        cost_estimate=pl.CostEstimate(
            flops=2 * span * weight.shape[0] * (depth + 4 * span),
            bytes_accessed=2 * weight.size + 6 * query.size + 6 * residual.size,
            transcendentals=heads * span * span,
        ),
    )(query, key, value, log_decay, doc_starts, residual, gain.reshape(1, depth), weight)
    return pl.pallas_call(
        write_kernel,
        out_shape=[jax.ShapeDtypeStruct((rows, depth), BF16)] * 2,
        in_specs=[vmem, vmem],
        out_specs=[hbm, hbm],
        scratch_shapes=[dma((2,))],
        cost_estimate=pl.CostEstimate(
            flops=0, bytes_accessed=8 * rows * depth, transcendentals=0
        ),
    )(*outs)


def solution(mesh):
    return jax.shard_map(
        functools.partial(shards, mesh.shape["seq"], mesh.shape["tp"]),
        mesh=mesh,
        in_specs=(
            P("seq", "tp"),
            P("seq", "tp"),
            P("seq", "tp"),
            P("tp", "seq"),
            P("seq", None),
            P(("seq", "tp"), None),
            P("tp", None),
            P(),
        ),
        out_specs=(P(("seq", "tp"), None), P(("seq", "tp"), None)),
        check_vma=False,
    )
```

```python
import functools

import jax
import jax.numpy as jnp
from jax import lax
from jax.experimental import pallas as pl
from jax.experimental.pallas import tpu as pltpu
from jax.sharding import PartitionSpec as P

MESH = pl.DeviceIdType.MESH
F32 = jnp.float32
BF16 = jnp.bfloat16
SKEW = 4


def _nt(a, b):
    return lax.dot_general(a, b, (((1,), (1,)), ((), ())), preferred_element_type=F32)


def _tn(a, b):
    return lax.dot_general(a, b, (((0,), (0,)), ((), ())), preferred_element_type=F32)


def kernel(
    cfg,
    q_hbm, k_hbm, v_hbm, decay_hbm, starts_hbm, res_hbm, gain_hbm, w_hbm,
    hid_ref, norm_ref,
    q_ref, k_ref, v_ref, decay_ref, starts_ref, res_ref, gain_ref, wbuf, decay_pad, cum_rows, bias, cum_cols, carry_cols, intra, att,
    state_out, sibling_in, pair_out, pair_in, prefix_out, prefix_in, carried,
    part, from_left, from_right, x_ref,
    in_sem, w_sem, s0_send, s0_recv, s1_send, s1_recv, s2_send, s2_recv, s3_send, s3_recv, rs_send, left_recv, right_recv,
):
    ns, nt, heads, hd, span, m, chunks, width, rows = cfg
    per = hd // m
    sets = state_out.shape[0]
    set_heads = heads // sets
    body_rows = set_heads * per
    group = 3 if set_heads % 3 == 0 else 1
    me = lax.axis_index("seq")
    pairs, half = ns // 2, m // 2
    pair, core = me // 2, me % 2
    sibling = me + 1 - 2 * core
    t = lax.axis_index("tp")

    pairs_of = [(decay_hbm, decay_ref), (starts_hbm, starts_ref)]
    for g in range(sets):
        lanes = pl.ds(g * set_heads * hd, set_heads * hd)
        pairs_of += [(k_hbm.at[:, lanes], k_ref.at[:, lanes]), (v_hbm.at[:, lanes], v_ref.at[:, lanes])]
    pairs_of += [(q_hbm, q_ref), (res_hbm, res_ref), (gain_hbm, gain_ref)]
    loads = [
        pltpu.make_async_copy(src, dst, in_sem.at[i]) for i, (src, dst) in enumerate(pairs_of)
    ]
    load_decay, load_starts, *load_sets, load_q, load_res, load_gain = loads
    for load in loads:
        load.start()

    def w_copy(c):
        return pltpu.make_async_copy(
            w_hbm.at[:, pl.ds(pl.multiple_of(c * width, width), width)], wbuf.at[c], w_sem.at[c]
        )

    barrier = pltpu.get_barrier_semaphore()
    pl.semaphore_signal(barrier, inc=1, device_id={"seq": sibling}, device_id_type=MESH)
    for d in range(1, pairs):
        pl.semaphore_signal(
            barrier, inc=1, device_id={"seq": lax.rem(me + 2 * d, ns)}, device_id_type=MESH
        )

    @pl.when(t > 0)
    def _():
        pl.semaphore_signal(barrier, inc=1, device_id={"tp": t - 1}, device_id_type=MESH)

    @pl.when(t < nt - 1)
    def _():
        pl.semaphore_signal(barrier, inc=1, device_id={"tp": t + 1}, device_id_type=MESH)

    row_i = lax.broadcasted_iota(jnp.int32, (span, span), 0)
    col_i = lax.broadcasted_iota(jnp.int32, (span, span), 1)
    lower = row_i >= col_i
    decay_pad[...] = jnp.zeros_like(decay_pad)
    load_decay.wait()
    decay_pad[0:heads, :] = decay_ref[...]
    cum = lax.dot_general(
        decay_pad[...], lower.astype(F32), (((1,), (1,)), ((), ())),
        preferred_element_type=F32, precision=lax.Precision.HIGHEST,
    )
    cum_rows[...] = cum
    cum_t = cum.T
    load_starts.wait()
    pos_c = lax.broadcasted_iota(jnp.int32, (span, 128), 0)
    seg_c = jnp.zeros((span, 128), jnp.int32)
    seg_r = jnp.zeros((1, span), jnp.int32)
    pos_r = lax.broadcasted_iota(jnp.int32, (1, span), 1)
    last_seg = jnp.zeros((1, 128), jnp.int32)
    for e in range(starts_ref.shape[1]):
        start = starts_ref[0, e]
        seg_c = seg_c + jnp.where(pos_c >= start, 1, 0)
        seg_r = seg_r + jnp.where(pos_r >= start, 1, 0)
        last_seg = last_seg + jnp.where(
            jnp.full((1, 128), span - 1, jnp.int32) >= start, 1, 0
        )
    tail_t = jnp.where(seg_c == last_seg, jnp.exp(cum_t[span - 1 : span, :] - cum_t), 0.0)
    carry_t = jnp.where(seg_c == 0, jnp.exp(cum_t), 0.0)

    through = jnp.where(last_seg == 0, jnp.exp(cum[:, span - 1 : span]), 0.0)[0:16, :]
    hi = through.astype(BF16)
    lo = (through - hi.astype(F32)).astype(BF16)

    def local_states(g):
        for i in range(set_heads):
            h = g * set_heads + i
            lanes = slice(h * hd, (h + 1) * hd)
            dk = (k_ref[:, lanes].astype(F32) * tail_t[:, h : h + 1]).astype(BF16)
            local = _tn(dk, v_ref[:, lanes]).astype(BF16)
            for j in range(m):
                state_out[g, j % 2, j // 2, i * per : (i + 1) * per, :] = local[
                    j * per : (j + 1) * per, :
                ]
        for j in range(m):
            state_out[g, j % 2, j // 2, body_rows : body_rows + 16, :] = hi
            state_out[g, j % 2, j // 2, body_rows + 16 : body_rows + 32, :] = lo

    def s0_copy(g, whole):
        src, dst = state_out.at[g], sibling_in.at[g]
        return pltpu.make_async_remote_copy(
            src_ref=src if whole else src.at[0], dst_ref=dst if whole else dst.at[0],
            send_sem=s0_send.at[g], recv_sem=s0_recv.at[g],
            device_id={"seq": sibling}, device_id_type=MESH,
        )

    def s1_copy(g, i, p):
        return pltpu.make_async_remote_copy(
            src_ref=pair_out.at[g, i], dst_ref=pair_in.at[g, p], send_sem=s1_send.at[g, i],
            recv_sem=s1_recv.at[g, p], device_id={"seq": 2 * i + core}, device_id_type=MESH,
        )

    def s2_copy(g, p, i):
        return pltpu.make_async_remote_copy(
            src_ref=prefix_out.at[g, p], dst_ref=prefix_in.at[g, core, i],
            send_sem=s2_send.at[g, p], recv_sem=s2_recv.at[g, i],
            device_id={"seq": 2 * p + core}, device_id_type=MESH,
        )

    def s3_copy(g, c):
        return pltpu.make_async_remote_copy(
            src_ref=prefix_in.at[g, c], dst_ref=prefix_in.at[g, c], send_sem=s3_send.at[g],
            recv_sem=s3_recv.at[g], device_id={"seq": sibling}, device_id_type=MESH,
        )

    def send_states(g):
        @pl.when(core == 0)
        def _():
            s0_copy(g, True).start()

        @pl.when(core == 1)
        def _():
            s0_copy(g, False).start()

    def decays(block):
        tail = block[body_rows : body_rows + 32, :].astype(F32)
        return tail[0:16] + tail[16:32]

    def totals(g):
        def work(first, second, parity):
            thr0, thr1 = decays(first[g, parity, 0]), decays(second[g, parity, 0])
            both = thr0 * thr1
            both_hi = both.astype(BF16)
            both_lo = (both - both_hi.astype(F32)).astype(BF16)
            for d in range(half):
                for i in range(set_heads):
                    h = g * set_heads + i
                    rows_h = slice(i * per, (i + 1) * per)
                    pair_out[g, d, rows_h, :] = (
                        thr1[h : h + 1, :] * first[g, parity, d, rows_h, :].astype(F32)
                        + second[g, parity, d, rows_h, :].astype(F32)
                    ).astype(BF16)
                pair_out[g, d, body_rows : body_rows + 16, :] = both_hi
                pair_out[g, d, body_rows + 16 : body_rows + 32, :] = both_lo

        @pl.when(core == 0)
        def _():
            s0_copy(g, False).wait_recv()
            work(state_out, sibling_in, 0)

        @pl.when(core == 1)
        def _():
            s0_copy(g, True).wait_recv()
            work(sibling_in, state_out, 1)

        for d in range(half):
            i = lax.rem(pair + d, half)

            @pl.when((i != pair) & (pair < pairs - 1))
            def _():
                s1_copy(g, i, pair).start()

        @pl.when((pair < half) & (pair < pairs - 1))
        def _():
            pair_in[g, pair] = pair_out[g, pair]

    for load in load_sets[0:2]:
        load.wait()
    local_states(0)
    pl.semaphore_wait(
        barrier, pairs + jnp.where(t > 0, 1, 0) + jnp.where(t < nt - 1, 1, 0)
    )
    send_states(0)
    for load in load_sets[2:]:
        load.wait()
    for c in range(chunks):
        w_copy(c).start()
    for g in range(1, sets):
        local_states(g)
        send_states(g)

    for g in range(sets):
        totals(g)

    seg_full = jnp.concatenate([seg_c] * (span // 128), axis=1)
    bias[...] = jnp.where(lower & (seg_full == seg_r), 0.0, -jnp.inf)
    for h in range(heads):
        cum_cols[h] = jnp.broadcast_to(cum_t[:, h : h + 1], (span, 128))
        carry_cols[h] = jnp.broadcast_to(carry_t[:, h : h + 1], (span, 128))
    load_q.wait()

    def within(i, _):
        for o in range(group):
            h = i * group + o
            lanes = pl.ds(pl.multiple_of(h * hd, hd), hd)
            scores = _nt(q_ref[:, lanes], k_ref[:, lanes])
            cols = jnp.concatenate([cum_cols[h]] * (span // 128), axis=1)
            decay = jnp.exp(cols - cum_rows[pl.ds(h, 1), :] + bias[...])
            weights = (scores * decay).astype(BF16)
            intra[h] = jnp.dot(weights, v_ref[:, lanes], preferred_element_type=F32)
        return 0

    def scan(g):
        @pl.when(pair < half)
        def _():
            state = [jnp.zeros((per, hd), F32) for _ in range(set_heads)]
            for p in range(pairs - 1):

                @pl.when(pair != p)
                def _():
                    s1_copy(g, 0, p).wait_recv()

                thr = decays(pair_in[g, p])
                for i in range(set_heads):
                    h = g * set_heads + i
                    rows_h = slice(i * per, (i + 1) * per)
                    state[i] = thr[h : h + 1, :] * state[i] + pair_in[g, p, rows_h, :].astype(F32)
                    prefix_out[g, p + 1, rows_h, :] = state[i].astype(BF16)

                @pl.when(pair != p + 1)
                def _():
                    s2_copy(g, p + 1, pair).start()

            @pl.when(pair > 0)
            def _():
                prefix_in[g, core, pair] = prefix_out[g, pair]

        @pl.when(pair == 0)
        def _():
            prefix_in[g] = jnp.zeros_like(prefix_in[g])

    def share(g):
        @pl.when(pair > 0)
        def _():
            for i in range(half):

                @pl.when(pair != i)
                def _():
                    s2_copy(g, 0, i).wait_recv()

            s3_copy(g, core).start()

    def across(g):
        @pl.when(pair > 0)
        def _():
            s3_copy(g, 1 - core).wait_recv()

        @pl.when(core == 0)
        def _():
            for j in range(m):
                carried[g, j] = prefix_in[g, j % 2, j // 2]

        @pl.when(core == 1)
        def _():
            thr = decays(sibling_in[g, 0, 0])
            for j in range(m):
                for i in range(set_heads):
                    h = g * set_heads + i
                    rows_h = slice(i * per, (i + 1) * per)
                    carried[g, j, rows_h, :] = (
                        thr[h : h + 1, :] * prefix_in[g, j % 2, j // 2, rows_h, :].astype(F32)
                        + sibling_in[g, j % 2, j // 2, rows_h, :].astype(F32)
                    ).astype(BF16)

        def some(n, _):
            for o in range(group):
                i = n * group + o
                h = g * set_heads + i
                lanes = pl.ds(pl.multiple_of(h * hd, hd), hd)
                rows_h = pl.ds(pl.multiple_of(i * per, per), per)
                state = jnp.concatenate([carried[g, j, rows_h, :] for j in range(m)], axis=0)
                inter = jnp.dot(q_ref[:, lanes], state, preferred_element_type=F32)
                mixed = intra[h] + inter * carry_cols[h]
                mean = jnp.mean(mixed * mixed, axis=1, keepdims=True)
                att[:, lanes] = (mixed * lax.rsqrt(mean + 1e-06)).astype(BF16)
            return 0

        lax.fori_loop(0, set_heads // group, some, 0)

    per_set = set_heads // group
    lax.fori_loop(0, per_set, within, 0)
    for g in range(sets):
        scan(g)
    lax.fori_loop(per_set, sets * per_set, within, 0)
    for g in range(sets):
        share(g)
    for g in range(sets):
        across(g)

    def right_copy(b, c):
        return pltpu.make_async_remote_copy(
            src_ref=part.at[b, c], dst_ref=from_left.at[b, c], send_sem=rs_send.at[b, c],
            recv_sem=left_recv.at[b, c], device_id={"tp": jnp.minimum(t + 1, nt - 1)},
            device_id_type=MESH,
        )

    def left_copy(b, c):
        return pltpu.make_async_remote_copy(
            src_ref=part.at[b, c], dst_ref=from_right.at[b, c], send_sem=rs_send.at[b, c],
            recv_sem=right_recv.at[b, c], device_id={"tp": jnp.maximum(t - 1, 0)},
            device_id_type=MESH,
        )

    units = (nt - 1) * chunks

    def add_into(b, c, other):
        part[b, c] = (part[b, c].astype(F32) + other[b, c].astype(F32)).astype(BF16)

    def step(k, _):
        @pl.when(k < chunks)
        def _():
            w_copy(k).wait()
            out = jnp.dot(att[...], wbuf[k], preferred_element_type=F32).astype(BF16)
            for b in range(nt):
                part[b, k] = out[b * rows : (b + 1) * rows, :]

        ur = k - t * SKEW
        br = nt - 1 - ur // chunks
        cr = ur % chunks

        @pl.when((ur >= 0) & (ur < units) & (br > t))
        def _():
            @pl.when(t > 0)
            def _():
                right_copy(br, cr).wait_recv()
                add_into(br, cr, from_left)

            right_copy(br, cr).start()

        ul = k - (nt - 1 - t) * SKEW
        bl = ul // chunks
        cl = ul % chunks

        @pl.when((ul >= 0) & (ul < units) & (bl < t))
        def _():
            @pl.when(t < nt - 1)
            def _():
                left_copy(bl, cl).wait_recv()
                add_into(bl, cl, from_right)

            left_copy(bl, cl).start()

        return 0

    lax.fori_loop(0, units + (nt - 1) * SKEW, step, 0)

    load_res.wait()
    load_gain.wait()

    total = jnp.zeros((rows, 1), F32)
    for c in range(chunks):
        lanes = slice(c * width, (c + 1) * width)
        x_ref[c] = res_ref[:, lanes].astype(F32) + part[t, c].astype(F32)

        @pl.when(t > 0)
        def _():
            right_copy(t, c).wait_recv()
            x_ref[c] += from_left[t, c].astype(F32)

        @pl.when(t < nt - 1)
        def _():
            left_copy(t, c).wait_recv()
            x_ref[c] += from_right[t, c].astype(F32)

        x = x_ref[c]
        hid_ref[:, lanes] = x.astype(BF16)
        total = total + jnp.sum(x * x, axis=1, keepdims=True)
    scale = lax.rsqrt(total / (chunks * width) + 1e-05)
    for c in range(chunks):
        lanes = slice(c * width, (c + 1) * width)
        norm_ref[:, lanes] = (x_ref[c] * scale * gain_ref[:, lanes]).astype(BF16)

    for g in range(sets):

        @pl.when(core == 0)
        def _():
            s0_copy(g, True).wait_send()

        @pl.when(core == 1)
        def _():
            s0_copy(g, False).wait_send()

        for i in range(half):

            @pl.when((pair != i) & (pair < pairs - 1))
            def _():
                s1_copy(g, i, 0).wait_send()

        for p in range(1, pairs):

            @pl.when((pair != p) & (pair < half))
            def _():
                s2_copy(g, p, 0).wait_send()

        @pl.when(pair > 0)
        def _():
            s3_copy(g, core).wait_send()

    def drain(u, _):
        b = u // chunks
        c = u % chunks

        @pl.when(b != t)
        def _():
            right_copy(b, c).wait_send()

        return 0

    lax.fori_loop(0, nt * chunks, drain, 0)


def shards(ns, nt, query, key, value, log_decay, doc_starts, residual, weight, gain):
    span = query.shape[0]
    heads = log_decay.shape[0]
    hd = query.shape[1] // heads
    rows, depth = residual.shape
    m = min(ns, hd // 16)
    pairs, half = ns // 2, m // 2
    per = hd // m
    sets = 2 if heads % 2 == 0 else 1
    body = heads // sets * per
    chunks = 16
    width = depth // chunks
    cfg = (ns, nt, heads, hd, span, m, chunks, width, rows)
    vmem = pl.BlockSpec(memory_space=pltpu.VMEM)
    hbm = pl.BlockSpec(memory_space=pl.ANY)
    dma = pltpu.SemaphoreType.DMA
    return pl.pallas_call(
        functools.partial(kernel, cfg),
        out_shape=[pltpu.VMEM((rows, depth), BF16)] * 2,
        in_specs=[hbm] * 8,
        out_specs=[vmem, vmem],
        scratch_shapes=[
            pltpu.VMEM(query.shape, BF16),
            pltpu.VMEM(query.shape, BF16),
            pltpu.VMEM(query.shape, BF16),
            pltpu.VMEM(log_decay.shape, F32),
            pltpu.SMEM(doc_starts.shape, jnp.int32),
            pltpu.VMEM(residual.shape, BF16),
            pltpu.VMEM((1, depth), F32),
            pltpu.VMEM((chunks, weight.shape[0], width), BF16),
            pltpu.VMEM((128, span), F32),
            pltpu.VMEM((128, span), F32),
            pltpu.VMEM((span, span), F32),
            pltpu.VMEM((heads, span, 128), F32),
            pltpu.VMEM((heads, span, 128), F32),
            pltpu.VMEM((heads, span, hd), F32),
            pltpu.VMEM((span, heads * hd), BF16),
            pltpu.VMEM((sets, 2, half, body + 32, hd), BF16),
            pltpu.VMEM((sets, 2, half, body + 32, hd), BF16),
            pltpu.VMEM((sets, half, body + 32, hd), BF16),
            pltpu.VMEM((sets, pairs, body + 32, hd), BF16),
            pltpu.VMEM((sets, pairs, body, hd), BF16),
            pltpu.VMEM((sets, 2, half, body, hd), BF16),
            pltpu.VMEM((sets, m, body, hd), BF16),
            pltpu.VMEM((nt, chunks, rows, width), BF16),
            pltpu.VMEM((nt, chunks, rows, width), BF16),
            pltpu.VMEM((nt, chunks, rows, width), BF16),
            pltpu.VMEM((chunks, rows, width), F32),
            dma((5 + 2 * sets,)),
            dma((chunks,)),
            dma((sets,)),
            dma((sets,)),
            dma((sets, half)),
            dma((sets, pairs)),
            dma((sets, pairs)),
            dma((sets, half)),
            dma((sets,)),
            dma((sets,)),
            dma((nt, chunks)),
            dma((nt, chunks)),
            dma((nt, chunks)),
        ],
        compiler_params=pltpu.CompilerParams(
            collective_id=0, has_side_effects=True, vmem_limit_bytes=56 * 1024 * 1024
        ),
        cost_estimate=pl.CostEstimate(
            flops=2 * span * weight.shape[0] * (depth + 4 * span),
            bytes_accessed=2 * weight.size + 6 * query.size + 6 * residual.size,
            transcendentals=heads * span * span,
        ),
    )(query, key, value, log_decay, doc_starts, residual, gain.reshape(1, depth), weight)


def solution(mesh):
    return jax.shard_map(
        functools.partial(shards, mesh.shape["seq"], mesh.shape["tp"]),
        mesh=mesh,
        in_specs=(
            P("seq", "tp"),
            P("seq", "tp"),
            P("seq", "tp"),
            P("tp", "seq"),
            P("seq", None),
            P(("seq", "tp"), None),
            P("tp", None),
            P(),
        ),
        out_specs=(P(("seq", "tp"), None), P(("seq", "tp"), None)),
        check_vma=False,
    )
```

```python
import functools

import jax
import jax.numpy as jnp
from jax import lax
from jax.experimental import pallas as pl
from jax.experimental.pallas import tpu as pltpu
from jax.sharding import PartitionSpec as P

MESH = pl.DeviceIdType.MESH
F32 = jnp.float32
BF16 = jnp.bfloat16
SKEW = 2


def _nt(a, b):
    return lax.dot_general(a, b, (((1,), (1,)), ((), ())), preferred_element_type=F32)


def _tn(a, b):
    return lax.dot_general(a, b, (((0,), (0,)), ((), ())), preferred_element_type=F32)


def kernel(
    cfg,
    q_hbm, k_hbm, v_hbm, decay_hbm, starts_hbm, res_hbm, gain_hbm, w_hbm,
    hid_ref, norm_ref,
    q_ref, k_ref, v_ref, decay_ref, starts_ref, res_ref, gain_ref, wbuf, decay_pad, cum_rows, bias, cum_cols, carry_cols, intra, att,
    state_out, sibling_in, pair_out, pair_in, prefix_out, prefix_in, carried,
    part, from_left, from_right, x_ref,
    in_sem, w_sem, s0_send, s0_recv, s1_send, s1_recv, s2_send, s2_recv, s3_send, s3_recv, rs_send, left_recv, right_recv,
):
    ns, nt, heads, hd, span, m, chunks, width, rows = cfg
    per = hd // m
    sets = state_out.shape[0]
    set_heads = heads // sets
    body_rows = set_heads * per
    group = 3 if set_heads % 3 == 0 else 1
    me = lax.axis_index("seq")
    pairs, half = ns // 2, m // 2
    pair, core = me // 2, me % 2
    sibling = me + 1 - 2 * core
    t = lax.axis_index("tp")

    pairs_of = [(decay_hbm, decay_ref), (starts_hbm, starts_ref)]
    for g in range(sets):
        lanes = pl.ds(g * set_heads * hd, set_heads * hd)
        pairs_of += [(k_hbm.at[:, lanes], k_ref.at[:, lanes]), (v_hbm.at[:, lanes], v_ref.at[:, lanes])]
    pairs_of += [(q_hbm, q_ref), (res_hbm, res_ref), (gain_hbm, gain_ref)]
    loads = [
        pltpu.make_async_copy(src, dst, in_sem.at[i]) for i, (src, dst) in enumerate(pairs_of)
    ]
    load_decay, load_starts, *load_sets, load_q, load_res, load_gain = loads
    for load in loads:
        load.start()

    def w_copy(c):
        return pltpu.make_async_copy(
            w_hbm.at[:, pl.ds(pl.multiple_of(c * width, width), width)], wbuf.at[c], w_sem.at[c]
        )

    barrier = pltpu.get_barrier_semaphore()
    pl.semaphore_signal(barrier, inc=1, device_id={"seq": sibling}, device_id_type=MESH)
    for d in range(1, pairs):
        pl.semaphore_signal(
            barrier, inc=1, device_id={"seq": lax.rem(me + 2 * d, ns)}, device_id_type=MESH
        )

    @pl.when(t > 0)
    def _():
        pl.semaphore_signal(barrier, inc=1, device_id={"tp": t - 1}, device_id_type=MESH)

    @pl.when(t < nt - 1)
    def _():
        pl.semaphore_signal(barrier, inc=1, device_id={"tp": t + 1}, device_id_type=MESH)

    row_i = lax.broadcasted_iota(jnp.int32, (span, span), 0)
    col_i = lax.broadcasted_iota(jnp.int32, (span, span), 1)
    lower = row_i >= col_i
    decay_pad[...] = jnp.zeros_like(decay_pad)
    load_decay.wait()
    decay_pad[0:heads, :] = decay_ref[...]
    cum = lax.dot_general(
        decay_pad[...], lower.astype(F32), (((1,), (1,)), ((), ())),
        preferred_element_type=F32, precision=lax.Precision.HIGHEST,
    )
    cum_rows[...] = cum
    cum_t = cum.T
    load_starts.wait()
    pos_c = lax.broadcasted_iota(jnp.int32, (span, 128), 0)
    seg_c = jnp.zeros((span, 128), jnp.int32)
    seg_r = jnp.zeros((1, span), jnp.int32)
    pos_r = lax.broadcasted_iota(jnp.int32, (1, span), 1)
    last_seg = jnp.zeros((1, 128), jnp.int32)
    for e in range(starts_ref.shape[1]):
        start = starts_ref[0, e]
        seg_c = seg_c + jnp.where(pos_c >= start, 1, 0)
        seg_r = seg_r + jnp.where(pos_r >= start, 1, 0)
        last_seg = last_seg + jnp.where(
            jnp.full((1, 128), span - 1, jnp.int32) >= start, 1, 0
        )
    tail_t = jnp.where(seg_c == last_seg, jnp.exp(cum_t[span - 1 : span, :] - cum_t), 0.0)
    carry_t = jnp.where(seg_c == 0, jnp.exp(cum_t), 0.0)

    through = jnp.where(last_seg == 0, jnp.exp(cum[:, span - 1 : span]), 0.0)[0:16, :]
    hi = through.astype(BF16)
    lo = (through - hi.astype(F32)).astype(BF16)

    def local_states(g):
        for i in range(set_heads):
            h = g * set_heads + i
            lanes = slice(h * hd, (h + 1) * hd)
            dk = (k_ref[:, lanes].astype(F32) * tail_t[:, h : h + 1]).astype(BF16)
            local = _tn(dk, v_ref[:, lanes]).astype(BF16)
            for j in range(m):
                state_out[g, j % 2, j // 2, i * per : (i + 1) * per, :] = local[
                    j * per : (j + 1) * per, :
                ]
        for j in range(m):
            state_out[g, j % 2, j // 2, body_rows : body_rows + 16, :] = hi
            state_out[g, j % 2, j // 2, body_rows + 16 : body_rows + 32, :] = lo

    def s0_copy(g, whole):
        src, dst = state_out.at[g], sibling_in.at[g]
        return pltpu.make_async_remote_copy(
            src_ref=src if whole else src.at[0], dst_ref=dst if whole else dst.at[0],
            send_sem=s0_send.at[g], recv_sem=s0_recv.at[g],
            device_id={"seq": sibling}, device_id_type=MESH,
        )

    def s1_copy(g, i, p):
        return pltpu.make_async_remote_copy(
            src_ref=pair_out.at[g, i], dst_ref=pair_in.at[g, p], send_sem=s1_send.at[g, i],
            recv_sem=s1_recv.at[g, p], device_id={"seq": 2 * i + core}, device_id_type=MESH,
        )

    def s2_copy(g, p, i):
        return pltpu.make_async_remote_copy(
            src_ref=prefix_out.at[g, p], dst_ref=prefix_in.at[g, core, i],
            send_sem=s2_send.at[g, p], recv_sem=s2_recv.at[g, i],
            device_id={"seq": 2 * p + core}, device_id_type=MESH,
        )

    def s3_copy(g, c):
        return pltpu.make_async_remote_copy(
            src_ref=prefix_in.at[g, c], dst_ref=prefix_in.at[g, c], send_sem=s3_send.at[g],
            recv_sem=s3_recv.at[g], device_id={"seq": sibling}, device_id_type=MESH,
        )

    def send_states(g):
        @pl.when(core == 0)
        def _():
            s0_copy(g, True).start()

        @pl.when(core == 1)
        def _():
            s0_copy(g, False).start()

    def decays(block):
        tail = block[body_rows : body_rows + 32, :].astype(F32)
        return tail[0:16] + tail[16:32]

    def totals(g):
        def work(first, second, parity):
            thr0, thr1 = decays(first[g, parity, 0]), decays(second[g, parity, 0])
            both = thr0 * thr1
            both_hi = both.astype(BF16)
            both_lo = (both - both_hi.astype(F32)).astype(BF16)
            for d in range(half):
                for i in range(set_heads):
                    h = g * set_heads + i
                    rows_h = slice(i * per, (i + 1) * per)
                    pair_out[g, d, rows_h, :] = (
                        thr1[h : h + 1, :] * first[g, parity, d, rows_h, :].astype(F32)
                        + second[g, parity, d, rows_h, :].astype(F32)
                    ).astype(BF16)
                pair_out[g, d, body_rows : body_rows + 16, :] = both_hi
                pair_out[g, d, body_rows + 16 : body_rows + 32, :] = both_lo

        @pl.when(core == 0)
        def _():
            s0_copy(g, False).wait_recv()
            work(state_out, sibling_in, 0)

        @pl.when(core == 1)
        def _():
            s0_copy(g, True).wait_recv()
            work(sibling_in, state_out, 1)

        for d in range(half):
            i = lax.rem(pair + d, half)

            @pl.when((i != pair) & (pair < pairs - 1))
            def _():
                s1_copy(g, i, pair).start()

        @pl.when((pair < half) & (pair < pairs - 1))
        def _():
            pair_in[g, pair] = pair_out[g, pair]

    for load in load_sets[0:2]:
        load.wait()
    local_states(0)
    pl.semaphore_wait(
        barrier, pairs + jnp.where(t > 0, 1, 0) + jnp.where(t < nt - 1, 1, 0)
    )
    send_states(0)
    for load in load_sets[2:]:
        load.wait()
    for c in range(chunks):
        w_copy(c).start()
    for g in range(1, sets):
        local_states(g)
        send_states(g)

    for g in range(sets):
        totals(g)

    seg_full = jnp.concatenate([seg_c] * (span // 128), axis=1)
    bias[...] = jnp.where(lower & (seg_full == seg_r), 0.0, -jnp.inf)
    for h in range(heads):
        cum_cols[h] = jnp.broadcast_to(cum_t[:, h : h + 1], (span, 128))
        carry_cols[h] = jnp.broadcast_to(carry_t[:, h : h + 1], (span, 128))
    load_q.wait()

    def within(i, _):
        for o in range(group):
            h = i * group + o
            lanes = pl.ds(pl.multiple_of(h * hd, hd), hd)
            cum_row = cum_rows[pl.ds(h, 1), :]
            for top in range(0, span, 128):
                mine, seen = slice(top, top + 128), slice(0, top + 128)
                scores = _nt(q_ref[mine, lanes], k_ref[seen, lanes])
                cols = jnp.concatenate([cum_cols[h, mine, :]] * (top // 128 + 1), axis=1)
                decay = jnp.exp(cols - cum_row[:, seen] + bias[mine, seen])
                weights = (scores * decay).astype(BF16)
                intra[h, mine, :] = jnp.dot(
                    weights, v_ref[seen, lanes], preferred_element_type=F32
                )
        return 0

    def scan(g):
        @pl.when(pair < half)
        def _():
            state = [jnp.zeros((per, hd), F32) for _ in range(set_heads)]
            for p in range(pairs - 1):

                @pl.when(pair != p)
                def _():
                    s1_copy(g, 0, p).wait_recv()

                thr = decays(pair_in[g, p])
                for i in range(set_heads):
                    h = g * set_heads + i
                    rows_h = slice(i * per, (i + 1) * per)
                    state[i] = thr[h : h + 1, :] * state[i] + pair_in[g, p, rows_h, :].astype(F32)
                    prefix_out[g, p + 1, rows_h, :] = state[i].astype(BF16)

                @pl.when(pair != p + 1)
                def _():
                    s2_copy(g, p + 1, pair).start()

            @pl.when(pair > 0)
            def _():
                prefix_in[g, core, pair] = prefix_out[g, pair]

        @pl.when(pair == 0)
        def _():
            prefix_in[g] = jnp.zeros_like(prefix_in[g])

    def share(g):
        @pl.when(pair > 0)
        def _():
            for i in range(half):

                @pl.when(pair != i)
                def _():
                    s2_copy(g, 0, i).wait_recv()

            s3_copy(g, core).start()

    def across(g):
        @pl.when(pair > 0)
        def _():
            s3_copy(g, 1 - core).wait_recv()

        @pl.when(core == 0)
        def _():
            for j in range(m):
                carried[g, j] = prefix_in[g, j % 2, j // 2]

        @pl.when(core == 1)
        def _():
            thr = decays(sibling_in[g, 0, 0])
            for j in range(m):
                for i in range(set_heads):
                    h = g * set_heads + i
                    rows_h = slice(i * per, (i + 1) * per)
                    carried[g, j, rows_h, :] = (
                        thr[h : h + 1, :] * prefix_in[g, j % 2, j // 2, rows_h, :].astype(F32)
                        + sibling_in[g, j % 2, j // 2, rows_h, :].astype(F32)
                    ).astype(BF16)

        def some(n, _):
            for o in range(group):
                i = n * group + o
                h = g * set_heads + i
                lanes = pl.ds(pl.multiple_of(h * hd, hd), hd)
                rows_h = pl.ds(pl.multiple_of(i * per, per), per)
                state = jnp.concatenate([carried[g, j, rows_h, :] for j in range(m)], axis=0)
                inter = jnp.dot(q_ref[:, lanes], state, preferred_element_type=F32)
                mixed = intra[h] + inter * carry_cols[h]
                mean = jnp.mean(mixed * mixed, axis=1, keepdims=True)
                att[:, lanes] = (mixed * lax.rsqrt(mean + 1e-06)).astype(BF16)
            return 0

        lax.fori_loop(0, set_heads // group, some, 0)

    per_set = set_heads // group
    lax.fori_loop(0, per_set, within, 0)
    for g in range(sets):
        scan(g)
    lax.fori_loop(per_set, sets * per_set, within, 0)
    for g in range(sets):
        share(g)
    for g in range(sets):
        across(g)

    def right_copy(b, c):
        return pltpu.make_async_remote_copy(
            src_ref=part.at[b, c], dst_ref=from_left.at[b, c], send_sem=rs_send.at[b, c],
            recv_sem=left_recv.at[b, c], device_id={"tp": jnp.minimum(t + 1, nt - 1)},
            device_id_type=MESH,
        )

    def left_copy(b, c):
        return pltpu.make_async_remote_copy(
            src_ref=part.at[b, c], dst_ref=from_right.at[b, c], send_sem=rs_send.at[b, c],
            recv_sem=right_recv.at[b, c], device_id={"tp": jnp.maximum(t - 1, 0)},
            device_id_type=MESH,
        )

    units = (nt - 1) * chunks

    def add_into(b, c, other):
        part[b, c] = (part[b, c].astype(F32) + other[b, c].astype(F32)).astype(BF16)

    def step(k, _):
        @pl.when(k < chunks)
        def _():
            w_copy(k).wait()
            out = jnp.dot(att[...], wbuf[k], preferred_element_type=F32).astype(BF16)
            for b in range(nt):
                part[b, k] = out[b * rows : (b + 1) * rows, :]

        ur = k - t * SKEW
        br = nt - 1 - ur // chunks
        cr = ur % chunks

        @pl.when((ur >= 0) & (ur < units) & (br > t))
        def _():
            @pl.when(t > 0)
            def _():
                right_copy(br, cr).wait_recv()
                add_into(br, cr, from_left)

            right_copy(br, cr).start()

        ul = k - (nt - 1 - t) * SKEW
        bl = ul // chunks
        cl = ul % chunks

        @pl.when((ul >= 0) & (ul < units) & (bl < t))
        def _():
            @pl.when(t < nt - 1)
            def _():
                left_copy(bl, cl).wait_recv()
                add_into(bl, cl, from_right)

            left_copy(bl, cl).start()

        return 0

    lax.fori_loop(0, units + (nt - 1) * SKEW, step, 0)

    load_res.wait()
    load_gain.wait()

    total = jnp.zeros((rows, 1), F32)
    for c in range(chunks):
        lanes = slice(c * width, (c + 1) * width)
        x_ref[c] = res_ref[:, lanes].astype(F32) + part[t, c].astype(F32)

        @pl.when(t > 0)
        def _():
            right_copy(t, c).wait_recv()
            x_ref[c] += from_left[t, c].astype(F32)

        @pl.when(t < nt - 1)
        def _():
            left_copy(t, c).wait_recv()
            x_ref[c] += from_right[t, c].astype(F32)

        x = x_ref[c]
        hid_ref[:, lanes] = x.astype(BF16)
        total = total + jnp.sum(x * x, axis=1, keepdims=True)
    scale = lax.rsqrt(total / (chunks * width) + 1e-05)
    for c in range(chunks):
        lanes = slice(c * width, (c + 1) * width)
        norm_ref[:, lanes] = (x_ref[c] * scale * gain_ref[:, lanes]).astype(BF16)

    for g in range(sets):

        @pl.when(core == 0)
        def _():
            s0_copy(g, True).wait_send()

        @pl.when(core == 1)
        def _():
            s0_copy(g, False).wait_send()

        for i in range(half):

            @pl.when((pair != i) & (pair < pairs - 1))
            def _():
                s1_copy(g, i, 0).wait_send()

        for p in range(1, pairs):

            @pl.when((pair != p) & (pair < half))
            def _():
                s2_copy(g, p, 0).wait_send()

        @pl.when(pair > 0)
        def _():
            s3_copy(g, core).wait_send()

    def drain(u, _):
        b = u // chunks
        c = u % chunks

        @pl.when(b != t)
        def _():
            right_copy(b, c).wait_send()

        return 0

    lax.fori_loop(0, nt * chunks, drain, 0)


def shards(ns, nt, query, key, value, log_decay, doc_starts, residual, weight, gain):
    span = query.shape[0]
    heads = log_decay.shape[0]
    hd = query.shape[1] // heads
    rows, depth = residual.shape
    m = min(ns, hd // 16)
    pairs, half = ns // 2, m // 2
    per = hd // m
    sets = 2 if heads % 2 == 0 else 1
    body = heads // sets * per
    chunks = 8
    width = depth // chunks
    cfg = (ns, nt, heads, hd, span, m, chunks, width, rows)
    vmem = pl.BlockSpec(memory_space=pltpu.VMEM)
    hbm = pl.BlockSpec(memory_space=pl.ANY)
    dma = pltpu.SemaphoreType.DMA
    return pl.pallas_call(
        functools.partial(kernel, cfg),
        out_shape=[pltpu.VMEM((rows, depth), BF16)] * 2,
        in_specs=[hbm] * 8,
        out_specs=[vmem, vmem],
        scratch_shapes=[
            pltpu.VMEM(query.shape, BF16),
            pltpu.VMEM(query.shape, BF16),
            pltpu.VMEM(query.shape, BF16),
            pltpu.VMEM(log_decay.shape, F32),
            pltpu.SMEM(doc_starts.shape, jnp.int32),
            pltpu.VMEM(residual.shape, BF16),
            pltpu.VMEM((1, depth), F32),
            pltpu.VMEM((chunks, weight.shape[0], width), BF16),
            pltpu.VMEM((128, span), F32),
            pltpu.VMEM((128, span), F32),
            pltpu.VMEM((span, span), F32),
            pltpu.VMEM((heads, span, 128), F32),
            pltpu.VMEM((heads, span, 128), F32),
            pltpu.VMEM((heads, span, hd), F32),
            pltpu.VMEM((span, heads * hd), BF16),
            pltpu.VMEM((sets, 2, half, body + 32, hd), BF16),
            pltpu.VMEM((sets, 2, half, body + 32, hd), BF16),
            pltpu.VMEM((sets, half, body + 32, hd), BF16),
            pltpu.VMEM((sets, pairs, body + 32, hd), BF16),
            pltpu.VMEM((sets, pairs, body, hd), BF16),
            pltpu.VMEM((sets, 2, half, body, hd), BF16),
            pltpu.VMEM((sets, m, body, hd), BF16),
            pltpu.VMEM((nt, chunks, rows, width), BF16),
            pltpu.VMEM((nt, chunks, rows, width), BF16),
            pltpu.VMEM((nt, chunks, rows, width), BF16),
            pltpu.VMEM((chunks, rows, width), F32),
            dma((5 + 2 * sets,)),
            dma((chunks,)),
            dma((sets,)),
            dma((sets,)),
            dma((sets, half)),
            dma((sets, pairs)),
            dma((sets, pairs)),
            dma((sets, half)),
            dma((sets,)),
            dma((sets,)),
            dma((nt, chunks)),
            dma((nt, chunks)),
            dma((nt, chunks)),
        ],
        compiler_params=pltpu.CompilerParams(
            collective_id=0, has_side_effects=True, vmem_limit_bytes=56 * 1024 * 1024
        ),
        cost_estimate=pl.CostEstimate(
            flops=2 * span * weight.shape[0] * (depth + 4 * span),
            bytes_accessed=2 * weight.size + 6 * query.size + 6 * residual.size,
            transcendentals=heads * span * span,
        ),
    )(query, key, value, log_decay, doc_starts, residual, gain.reshape(1, depth), weight)


def solution(mesh):
    return jax.shard_map(
        functools.partial(shards, mesh.shape["seq"], mesh.shape["tp"]),
        mesh=mesh,
        in_specs=(
            P("seq", "tp"),
            P("seq", "tp"),
            P("seq", "tp"),
            P("tp", "seq"),
            P("seq", None),
            P(("seq", "tp"), None),
            P("tp", None),
            P(),
        ),
        out_specs=(P(("seq", "tp"), None), P(("seq", "tp"), None)),
        check_vma=False,
    )
```
